256 devices in a mesh: req: 64 (over z, x, core), head: 4 (over y).
Axes of the slice: x: 4, y: 4, z: 8, core: 2. Of those that a mesh axis runs over, the one named last changes fastest.
Arguments:
- latent_pages: bfloat16 [16384, 96, 512], P(('req', 'head')), may hold values from -6 to 6
- rope_pages: bfloat16 [16384, 6144], P(('req', 'head')), may hold values from -6 to 6
- page_place: int32 [16384], P('req'), may hold values from 0 to 255, as said below
- lengths: int32 [128], P('req'), may hold values from 1 to 12288
- q_latent: bfloat16 [128, 2, 128, 512], P('req', None, 'head'), may hold values from -6 to 6
- q_rope: bfloat16 [128, 2, 128, 64], P('req', None, 'head'), may hold values from -220 to 220
- new_latent: bfloat16 [128, 2, 512], P('req'), may hold values from -6 to 6
- new_rope: bfloat16 [128, 2, 64], P('req'), may hold values from -4 to 4
Outputs:
- head_out: bfloat16 [128, 2, 128, 512], P('req', None, 'head')
The draws below stay inside these ranges and needn't reach their ends.
Inputs may be any that keep to these rules, and one draw needn't show every extreme that they name: `page_place`: within each block of 256 entries every value 0 to 255 appears once.
All inputs are finite; a program needn't handle non-finite values.
Results may differ from the reference program's by a relative error of at most 0.008.
Values may be sent and summed in bfloat16 or wider, within the bound.
No kernel may reach another device: no remote copies, remote signals or barrier semaphores. Data moves between devices by JAX's collectives and lax.ppermute only.
A program may use at most 128 MiB of HBM per device.

```python
import jax
import jax.numpy as jnp
from jax import lax

HEADS = 128
LATENT = 512
ROPE = 64
NOPE = 128
STEPS = 2
PAGE = 96
PAGES_REQ = 128
REQ_DEV = 2
REQUESTS = 128
CTX = 12288
P_OWN = 256
PER_PEER = 1
PAGES = 16384
N_REQ = 64
N_HEAD = 4


def rope_keys(key):
    base = jax.random.normal(key, (REQUESTS, STEPS, ROPE), jnp.float32)
    base = jnp.clip(base, -4.0, 4.0)
    later = base[:, 1:2, :]
    former = base[:, 0:1, :]
    return jnp.concatenate([former, later], axis=1)


def draw_new_rope(key, part):
    return rope_keys(key).astype(jnp.bfloat16)


def draw_q_rope(key, part):
    key = jax.random.fold_in(key, 7)
    key_noise = jax.random.fold_in(key, 0)
    values = jnp.clip(jax.random.normal(key_noise, (REQUESTS, STEPS, HEADS, ROPE), jnp.float32), -6.0, 6.0)
    return values.astype(jnp.bfloat16)


def draw_page_place(key, part):
    key = jax.random.fold_in(key, 3)
    owner_keys = jax.random.split(key, PAGES // P_OWN)

    def shuffle_one(owner_key):
        return jax.random.permutation(owner_key, P_OWN)
    return jax.vmap(shuffle_one)(owner_keys).reshape(PAGES).astype(jnp.int32)


def draw_lengths(key, part):
    key = jax.random.fold_in(key, 9)
    key_len, key_spot = jax.random.split(key)
    values = jax.random.randint(key_len, (REQUESTS,), 1, CTX + 1)
    spot = jax.random.randint(key_spot, (), 0, REQUESTS)
    values = values.at[spot].set(CTX)
    values = values.at[(spot + 1) % REQUESTS].set(1)
    return values.astype(jnp.int32)


def steps_of(rng, shape, cuts, low, top_value):
    def one(position, blocks):
        steps = jax.random.uniform(jax.random.fold_in(jax.random.fold_in(rng, 6), position), (blocks,), jnp.float32, low / len(cuts), top_value / len(cuts))
        return jnp.repeat(jnp.exp(steps), shape[position] // blocks).reshape((-1,) + (1,) * (len(shape) - position - 1))

    factor_of = one(*cuts[0])
    for cut in cuts[1:]:
        factor_of = factor_of * one(*cut)
    return factor_of


def scatter_about(rng, shape, width, most, cuts=(), kind=jnp.bfloat16):
    level = steps_of(rng, shape, cuts, -0.22, 0.18) if cuts else 1.0
    drawn = jax.random.normal(rng, shape, jnp.float32) * width * level
    return jnp.minimum(jnp.maximum(drawn, -most), most).astype(kind)


def setup_inputs(seed: int = 0) -> dict:
    splits = jax.random.split(jax.random.key(seed), 9)
    return {
        "latent_pages": scatter_about(splits[0], (PAGES, PAGE, LATENT), 1.0, 6.0, ((0, 256),)),
        "rope_pages": scatter_about(splits[1], (PAGES, PAGE * ROPE), 1.0, 6.0, ((0, 256),)),
        "page_place": draw_page_place(jax.random.fold_in(splits[8], 71), 0),
        "lengths": draw_lengths(jax.random.fold_in(splits[8], 71), 0),
        "q_latent": scatter_about(splits[4], (REQUESTS, STEPS, HEADS, LATENT), 1.0, 6.0, ((0, 64), (2, 4))),
        "q_rope": draw_q_rope(jax.random.fold_in(splits[8], 71), 0),
        "new_latent": scatter_about(splits[6], (REQUESTS, STEPS, LATENT), 1.0, 6.0, ((0, 64),)),
        "new_rope": draw_new_rope(jax.random.fold_in(splits[8], 71), 0),
    }


NEG = -1.0e30


def contract(left, right):
    return lax.dot_general(left, right, (((1,), (1,)), ((), ())), preferred_element_type=jnp.float32)


def softmax_part(latent_rows, rope_rows, key_mask, query_lat, query_rope, fresh_lat, fresh_rope, fresh_mask, scaling):
    score = (contract(query_lat, latent_rows) + contract(query_rope, rope_rows)) * scaling
    fresh = (contract(query_lat, fresh_lat) + contract(query_rope, fresh_rope)) * scaling
    score = jnp.where(key_mask[None, :], score, NEG)
    fresh = jnp.where(fresh_mask, fresh, NEG)
    maxima = jnp.maximum(jnp.max(score, axis=1), jnp.max(fresh, axis=1))
    weight = jnp.where(key_mask[None, :], jnp.exp(score - maxima[:, None]), 0.0)
    weight_new = jnp.where(fresh_mask, jnp.exp(fresh - maxima[:, None]), 0.0)
    totals = jnp.sum(weight, axis=1) + jnp.sum(weight_new, axis=1)
    weighted = jnp.dot(weight.astype(jnp.bfloat16), latent_rows, preferred_element_type=jnp.float32)
    weighted = weighted + jnp.dot(weight_new.astype(jnp.bfloat16), fresh_lat, preferred_element_type=jnp.float32)
    return maxima, totals, weighted


def fresh_allowed(step_count, head_count):
    row_step = jnp.arange(step_count * head_count, dtype=jnp.int32) // head_count
    return jnp.arange(step_count, dtype=jnp.int32)[None, :] <= row_step[:, None]


def reference(latent_pages, rope_pages, page_place, lengths, q_latent, q_rope, new_latent, new_rope):
    scaling = float(NOPE + ROPE) ** -0.5
    latent_view = latent_pages.reshape(N_REQ, N_HEAD, N_REQ, PER_PEER, PAGE, LATENT)
    rope_view = rope_pages.reshape(N_REQ, N_HEAD, N_REQ, PER_PEER, PAGE * ROPE)
    fresh_mask = fresh_allowed(STEPS, HEADS)

    def one_owner(owner):
        owned = jnp.take(latent_view, owner, axis=2)
        owned = jnp.transpose(owned, (1, 0, 2, 3, 4)).reshape(P_OWN, PAGE, LATENT)
        owned_rope = jnp.take(rope_view, owner, axis=2)
        owned_rope = jnp.transpose(owned_rope, (1, 0, 2, 3)).reshape(P_OWN, PAGE * ROPE)
        place = lax.dynamic_slice_in_dim(page_place, owner * P_OWN, P_OWN)
        inverse = jnp.zeros((P_OWN,), jnp.int32).at[place].set(jnp.arange(P_OWN, dtype=jnp.int32))

        def one_request(request):
            slots = lax.dynamic_slice_in_dim(inverse, request * PAGES_REQ, PAGES_REQ)
            latent_rows = owned[slots].reshape(CTX, LATENT)
            rope_rows = owned_rope[slots].reshape(CTX, ROPE)
            global_req = owner * REQ_DEV + request
            key_mask = jnp.arange(CTX, dtype=jnp.int32) < lengths[global_req]
            query_lat = q_latent[global_req].reshape(STEPS * HEADS, LATENT)
            query_rope = q_rope[global_req].reshape(STEPS * HEADS, ROPE)
            maxima, totals, weighted = softmax_part(latent_rows, rope_rows, key_mask, query_lat, query_rope,
                                                    new_latent[global_req], new_rope[global_req], fresh_mask, scaling)
            return (weighted / totals[:, None]).astype(jnp.bfloat16).reshape(STEPS, HEADS, LATENT)

        return lax.map(one_request, jnp.arange(REQ_DEV, dtype=jnp.int32))

    result = lax.map(one_owner, jnp.arange(N_REQ, dtype=jnp.int32))
    return result.reshape(REQUESTS, STEPS, HEADS, LATENT)
```

```python
import functools

import jax
import jax.numpy as jnp
from jax import lax
from jax.experimental import pallas as pl
from jax.experimental.pallas import tpu as pltpu
from jax.sharding import PartitionSpec as P

ROPE = 64
NOPE = 128
SCALE = float(NOPE + ROPE) ** -0.5
NEG = -1e30

NZ, NX, NC, NY = 8, 4, 2, 4
AXES = ("req", "head")
PAIRS = NZ // 2
SLOTS = NZ * NX * NC
PAGE = 96
BLOCK = 4
TOKENS = BLOCK * PAGE
ROWS = 64
META = 16


def device_id(z, x, core, y):
    return ((z * NX + x) * NC + core) * NY + y


def page_groups():
    return [
        [
            device_id(2 * j + zo % 2, x, c, (zo // 2 + j) % NY)
            for zo in range(NZ)
            for x in range(NX)
            for c in range(NC)
        ]
        for j in range(PAIRS)
    ]


def home_pairs(d):
    pairs = []
    for z in range(NZ):
        for x in range(NX):
            for c in range(NC):
                for y in range(NY):
                    zo = 2 * ((y - z // 2) % PAIRS) + z % 2
                    pairs.append((device_id(z, x, c, y), device_id(zo, x, c, (y + d) % NY)))
    return pairs


def contract(left, right):
    return lax.dot_general(
        left, right, (((1,), (1,)), ((), ())), preferred_element_type=jnp.float32
    )


def attend_kernel(
    order_ref, valid_ref, count_ref, lat_ref, rope_ref, q0, q1, q2, q3, o0, o1, o2, o3,
    score_ref, acc_ref, total_ref
):
    queries, outs = (q0, q1, q2, q3), (o0, o1, o2, o3)
    token = lax.broadcasted_iota(jnp.int32, (TOKENS, TOKENS // 2), 0)
    pair = lax.broadcasted_iota(jnp.int32, (TOKENS, TOKENS // 2), 1)
    spread = (token // 2 == pair).astype(jnp.bfloat16)
    half = (
        lax.broadcasted_iota(jnp.int32, (TOKENS, 2 * ROPE), 0) % 2
        == lax.broadcasted_iota(jnp.int32, (TOKENS, 2 * ROPE), 1) // ROPE
    )
    lane = lax.broadcasted_iota(jnp.int32, (1, TOKENS), 1)
    sums = []
    for request in range(2):
        rows = slice(request * ROWS, (request + 1) * ROWS)
        query = jnp.concatenate([q[rows, :] for q in queries], axis=0)
        query_lat, query_rope = query[:, :512], query[:, 512:]
        start = count_ref[0] * request
        count = count_ref[request]
        blocks = (count + BLOCK - 1) // BLOCK

        def slot(block, index):
            return order_ref[jnp.minimum(start + block * BLOCK + index, SLOTS - 1)]

        def latents(block):
            return jnp.concatenate([lat_ref[slot(block, i)] for i in range(BLOCK)], axis=0)

        def score_block(block, maxima):
            keys = latents(block)
            pairs = jnp.concatenate([rope_ref[slot(block, i)] for i in range(BLOCK)], axis=0)
            spread_keys = jnp.dot(spread, pairs, preferred_element_type=jnp.float32)
            rope_keys = jnp.where(half, spread_keys, 0.0).astype(jnp.bfloat16)
            score = contract(query_lat, keys) + contract(query_rope, rope_keys)
            limit = jnp.zeros((1, TOKENS), jnp.int32)
            for i in range(BLOCK):
                place = block * BLOCK + i
                valid = valid_ref[jnp.minimum(start + place, SLOTS - 1)]
                valid = jnp.where(place < count, valid, 0)
                limit = jnp.where(lane >= i * PAGE, i * PAGE + valid, limit)
            score = score * SCALE + jnp.where(lane < limit, 0.0, NEG)
            score_ref[block] = score
            for i in range(TOKENS // 128):
                maxima = jnp.maximum(maxima, score[:, i * 128 : (i + 1) * 128])
            return maxima

        maxima = lax.fori_loop(
            0, blocks, score_block, jnp.full((4 * ROWS, 128), NEG, jnp.float32)
        )
        top = jnp.max(maxima, axis=1, keepdims=True)
        acc_ref[...] = jnp.zeros_like(acc_ref)
        total_ref[...] = jnp.zeros_like(total_ref)

        def weigh_block(block, carry):
            weight = jnp.exp(score_ref[block] - top)
            part = weight[:, :128]
            for i in range(1, TOKENS // 128):
                part = part + weight[:, i * 128 : (i + 1) * 128]
            total_ref[...] += part
            acc_ref[...] += jnp.dot(
                weight.astype(jnp.bfloat16), latents(block), preferred_element_type=jnp.float32
            )
            return carry

        lax.fori_loop(0, blocks, weigh_block, 0)
        total = jnp.sum(total_ref[...], axis=1, keepdims=True)
        total = jnp.where(total > 0.0, total, 1.0)
        result = (acc_ref[...] / total).astype(jnp.bfloat16)
        sums.append(top + jnp.log(total))
        for out, i in zip(outs, range(4)):
            out[rows, :] = result[i * ROWS : (i + 1) * ROWS, :]
    lane = lax.broadcasted_iota(jnp.int32, (4 * ROWS, 128), 1)
    meta = jnp.zeros((4 * ROWS, 128), jnp.float32)
    for request in range(2):
        rest = sums[request]
        for part in range(3):
            piece = rest.astype(jnp.bfloat16).astype(jnp.float32)
            meta = jnp.where(lane == request * 3 + part, piece, meta)
            rest = rest - piece
    meta = meta.astype(jnp.bfloat16)
    for out, i in zip(outs, range(4)):
        part = meta[i * ROWS : (i + 1) * ROWS, :]
        out[2 * ROWS :, :] = jnp.concatenate(
            [part[k * META : (k + 1) * META, :] for k in range(4)], axis=1
        )


def merge_kernel(p0, p1, p2, p3, query_ref, new_lat_ref, new_rope_ref, out_ref):
    parts = (p0, p1, p2, p3)
    meta = [
        jnp.concatenate(
            [p[2 * ROWS :, k * 128 : (k + 1) * 128] for k in range(4)], axis=0
        ).astype(jnp.float32)
        for p in parts
    ]
    first_step = lax.broadcasted_iota(jnp.int32, (ROWS, 1), 0) < ROWS // 2
    for request in range(2):
        rows = slice(request * ROWS, (request + 1) * ROWS)
        query = query_ref[rows, :].astype(jnp.float32)
        fresh = []
        for step in range(2):
            key = new_lat_ref[request, step : step + 1, :].astype(jnp.float32)
            rope = new_rope_ref[request, step : step + 1, :].astype(jnp.float32)
            score = jnp.sum(query[:, :512] * key, axis=1, keepdims=True)
            score = score + jnp.sum(query[:, 512 : 512 + ROPE] * rope, axis=1, keepdims=True)
            fresh.append((score * SCALE, key))
        later = jnp.where(first_step, NEG, fresh[1][0])
        fresh[1] = (later, fresh[1][1])
        sums = [
            m[:, 3 * request : 3 * request + 1]
            + m[:, 3 * request + 1 : 3 * request + 2]
            + m[:, 3 * request + 2 : 3 * request + 3]
            for m in meta
        ]
        top = functools.reduce(jnp.maximum, sums + [s for s, _ in fresh])
        total = jnp.zeros((ROWS, 1), jnp.float32)
        acc = jnp.zeros((ROWS, 512), jnp.float32)
        for p, s in zip(parts, sums):
            weight = jnp.exp(s - top)
            total = total + weight
            acc = acc + weight * p[rows, :].astype(jnp.float32)
        for score, key in fresh:
            weight = jnp.exp(score - top)
            total = total + weight
            acc = acc + weight.astype(jnp.bfloat16).astype(jnp.float32) * key
        out_ref[request] = (acc / total).astype(jnp.bfloat16)


def page_table(query, pair):
    row = query[2 * ROWS].astype(jnp.int32)
    slot = jnp.arange(SLOTS, dtype=jnp.int32)
    zo, xc = slot // (NX * NC), slot % (NX * NC)
    holder = (2 * pair + zo % 2) * (NX * NC) + xc
    place = row[((zo // 2 + pair) % NY) * SLOTS + holder]
    request = place // 128
    length = jnp.where(
        request == 0, row[256] * 128 + row[258], row[257] * 128 + row[259]
    )
    valid = jnp.clip(length - (place % 128) * PAGE, 0, PAGE)
    key = jnp.where(valid > 0, request, 2)
    before = (key[None, :] < key[:, None]) | (
        (key[None, :] == key[:, None]) & (slot[None, :] < slot[:, None])
    )
    rank = jnp.sum(before.astype(jnp.int32), axis=1)
    hit = rank[:, None] == slot[None, :]
    order = jnp.sum(jnp.where(hit, slot[:, None], 0), axis=0)
    valid = jnp.sum(jnp.where(hit, valid[:, None], 0), axis=0)
    count = jnp.stack([jnp.sum((key == r).astype(jnp.int32)) for r in range(2)])
    return order, valid, count


def on_device(
    latent_pages, rope_pages, page_place, lengths, q_latent, q_rope, new_latent, new_rope
):
    groups = page_groups()
    pair = lax.axis_index("req") // (2 * NX * NC)
    rope_keys = q_rope.reshape(2 * ROWS, ROPE)
    place = page_place.astype(jnp.bfloat16)
    length = jnp.concatenate([lengths // 128, lengths % 128]).astype(jnp.bfloat16)
    row = jnp.concatenate([place, length, jnp.zeros((640 - 260,), jnp.bfloat16)])
    query = jnp.concatenate([q_latent.reshape(2 * ROWS, 512), rope_keys, rope_keys], axis=1)
    query = jnp.concatenate(
        [query, row[None, :], jnp.zeros((META - 1, 640), jnp.bfloat16)], axis=0
    )
    queries = [
        lax.ppermute(query, AXES, [(b, a) for a, b in home_pairs(d)]) for d in range(4)
    ]
    exchange = functools.partial(
        lax.all_to_all,
        axis_name=AXES,
        split_axis=0,
        concat_axis=0,
        axis_index_groups=groups,
        tiled=True,
    )
    rope = exchange(rope_pages.reshape(SLOTS, PAGE // 2, 2 * ROPE))
    lat = exchange(latent_pages)
    order, valid, count = page_table(queries[0], pair)
    whole = pl.BlockSpec(memory_space=pltpu.VMEM)
    scalars = pl.BlockSpec(memory_space=pltpu.SMEM)
    partial = jax.ShapeDtypeStruct((2 * ROWS + META, 512), jnp.bfloat16)
    parts = pl.pallas_call(
        attend_kernel,
        out_shape=[partial] * 4,
        in_specs=[scalars] * 3 + [whole] * 6,
        out_specs=[whole] * 4,
        scratch_shapes=[
            pltpu.VMEM((SLOTS // BLOCK, 4 * ROWS, TOKENS), jnp.float32),
            pltpu.VMEM((4 * ROWS, 512), jnp.float32),
            pltpu.VMEM((4 * ROWS, 128), jnp.float32),
        ],
        compiler_params=pltpu.CompilerParams(vmem_limit_bytes=40 * 1024 * 1024),
        cost_estimate=pl.CostEstimate(
            flops=4 * ROWS * 6144 * 1152 * 2, bytes_accessed=8 << 20, transcendentals=1 << 20
        ),
        name="attend",
    )(order, valid, count, lat, rope, *queries)
    home = [lax.ppermute(part, AXES, home_pairs(d)) for d, part in enumerate(parts)]
    out = pl.pallas_call(
        merge_kernel,
        out_shape=jax.ShapeDtypeStruct((2, ROWS, 512), jnp.bfloat16),
        in_specs=[whole] * 7,
        out_specs=whole,
        name="merge",
    )(*home, query, new_latent, new_rope)
    return out.reshape(q_latent.shape)


def solution(mesh):
    return jax.shard_map(
        on_device,
        mesh=mesh,
        in_specs=(
            P(("req", "head"), None, None),
            P(("req", "head"), None),
            P("req"),
            P("req"),
            P("req", None, "head", None),
            P("req", None, "head", None),
            P("req", None, None),
            P("req", None, None),
        ),
        out_specs=P("req", None, "head", None),
        check_vma=False,
    )
```

```python
import functools

import jax
import jax.numpy as jnp
from jax import lax
from jax.experimental import pallas as pl
from jax.experimental.pallas import tpu as pltpu
from jax.sharding import PartitionSpec as P

ROPE = 64
NOPE = 128
SCALE = float(NOPE + ROPE) ** -0.5
NEG = -1e30

NZ, NX, NC, NY = 8, 4, 2, 4
AXES = ("req", "head")
PAIRS = NZ // 2
SLOTS = NZ * NX * NC
PAGE = 96
BLOCK = 8
TOKENS = BLOCK * PAGE
ROWS = 64
META = 16


def device_id(z, x, core, y):
    return ((z * NX + x) * NC + core) * NY + y


def served_pair(pair, y, core):
    shift = y + 2 * (pair % 2)
    return (pair + (1 - 2 * core) * shift) % PAIRS


def serving_y(owner_pair, pair, core):
    return ((1 - 2 * core) * (owner_pair - pair) - 2 * (pair % 2)) % NY


def devices():
    return [
        (z, x, c, y) for z in range(NZ) for x in range(NX) for c in range(NC) for y in range(NY)
    ]


def page_groups():
    return [
        [
            device_id(2 * j + zo % 2, x, c, serving_y(zo // 2, j, c))
            for zo in range(NZ)
            for x in range(NX)
            for c in range(NC)
        ]
        for j in range(PAIRS)
    ]


def home_pairs(d):
    return [
        (
            device_id(z, x, c, y),
            device_id(2 * served_pair(z // 2, y, c) + z % 2, x, c, (y + d) % NY),
        )
        for z, x, c, y in devices()
    ]


def contract(left, right):
    return lax.dot_general(
        left, right, (((1,), (1,)), ((), ())), preferred_element_type=jnp.float32
    )


def attend_kernel(
    order_ref, rope_order_ref, valid_ref, count_ref, lat_ref, rope_ref, query_ref,
    o0, o1, o2, o3, page_ref, score_ref, acc_ref, sems
):
    outs = (o0, o1, o2, o3)

    def copy(place):
        return pltpu.make_async_copy(
            lat_ref.at[order_ref[place]], page_ref.at[place], sems.at[place]
        )

    def begin(place, carry):
        copy(place).start()
        return carry

    lax.fori_loop(0, count_ref[0] + count_ref[1], begin, 0)
    token = lax.broadcasted_iota(jnp.int32, (TOKENS, TOKENS // 2), 0)
    pair = lax.broadcasted_iota(jnp.int32, (TOKENS, TOKENS // 2), 1)
    spread = (token // 2 == pair).astype(jnp.bfloat16)
    half = (
        lax.broadcasted_iota(jnp.int32, (TOKENS, 2 * ROPE), 0) % 2
        == lax.broadcasted_iota(jnp.int32, (TOKENS, 2 * ROPE), 1) // ROPE
    )
    lane = lax.broadcasted_iota(jnp.int32, (1, TOKENS), 1)
    meta_lane = lax.broadcasted_iota(jnp.int32, (4 * ROWS, 128), 1)
    meta = jnp.zeros((4 * ROWS, 128), jnp.float32)
    for request in range(2):
        rows = slice(request * ROWS, (request + 1) * ROWS)
        start = count_ref[0] * request
        count = count_ref[request]
        blocks = (count + BLOCK - 1) // BLOCK

        def place_of(block, index):
            return start + jnp.minimum(block * BLOCK + index, count - 1)

        def latents(block):
            return jnp.concatenate([page_ref[place_of(block, i)] for i in range(BLOCK)], axis=0)

        def score_block(block, maxima):
            for i in range(BLOCK):

                @pl.when(block * BLOCK + i < count)
                def _():
                    copy(start + block * BLOCK + i).wait()

            pairs = jnp.concatenate(
                [rope_ref[rope_order_ref[place_of(block, i)]] for i in range(BLOCK)], axis=0
            )
            spread_keys = jnp.dot(spread, pairs, preferred_element_type=jnp.float32)
            rope_keys = jnp.where(half, spread_keys, 0.0).astype(jnp.bfloat16)
            keys = jnp.concatenate([latents(block), rope_keys], axis=1)
            limit = jnp.zeros((1, TOKENS), jnp.int32)
            for i in range(BLOCK):
                valid = jnp.where(block * BLOCK + i < count, valid_ref[place_of(block, i)], 0)
                limit = jnp.where(lane >= i * PAGE, i * PAGE + valid, limit)
            score = contract(query_ref[request], keys) * SCALE + jnp.where(lane < limit, 0.0, NEG)
            score_ref[block] = score
            for i in range(TOKENS // 128):
                maxima = jnp.maximum(maxima, score[:, i * 128 : (i + 1) * 128])
            return maxima

        maxima = lax.fori_loop(
            0, blocks, score_block, jnp.full((4 * ROWS, 128), NEG, jnp.float32)
        )
        top = jnp.max(maxima, axis=1, keepdims=True)
        acc_ref[...] = jnp.zeros_like(acc_ref)

        def weigh_block(block, total):
            weight = jnp.exp(score_ref[block] - top)
            for i in range(TOKENS // 128):
                total = total + weight[:, i * 128 : (i + 1) * 128]
            acc_ref[...] += jnp.dot(
                weight.astype(jnp.bfloat16), latents(block), preferred_element_type=jnp.float32
            )
            return total

        total = lax.fori_loop(
            0, blocks, weigh_block, jnp.zeros((4 * ROWS, 128), jnp.float32)
        )
        total = jnp.sum(total, axis=1, keepdims=True)
        total = jnp.where(total > 0.0, total, 1.0)
        result = (acc_ref[...] / total).astype(jnp.bfloat16)
        for i, out in enumerate(outs):
            out[rows, :] = result[i * ROWS : (i + 1) * ROWS, :]
        rest = top + jnp.log(total)
        for part in range(3):
            piece = rest.astype(jnp.bfloat16).astype(jnp.float32)
            meta = jnp.where(meta_lane == request * 3 + part, piece, meta)
            rest = rest - piece
    meta = meta.astype(jnp.bfloat16)
    for i, out in enumerate(outs):
        part = meta[i * ROWS : (i + 1) * ROWS, :]
        out[2 * ROWS :, :] = jnp.concatenate(
            [part[k * META : (k + 1) * META, :] for k in range(4)], axis=1
        )


def merge_kernel(
    p0, p1, p2, p3, query_lat_ref, query_rope_ref, new_lat_ref, new_rope_ref, out_ref
):
    parts = (p0, p1, p2, p3)
    meta = [
        jnp.concatenate(
            [p[2 * ROWS :, k * 128 : (k + 1) * 128] for k in range(4)], axis=0
        ).astype(jnp.float32)
        for p in parts
    ]
    first_step = lax.broadcasted_iota(jnp.int32, (ROWS, 1), 0) < ROWS // 2
    for request in range(2):
        rows = slice(request * ROWS, (request + 1) * ROWS)
        query_lat = query_lat_ref[rows, :].astype(jnp.float32)
        query_rope = query_rope_ref[rows, :].astype(jnp.float32)
        fresh = []
        for step in range(2):
            key = new_lat_ref[request, step : step + 1, :].astype(jnp.float32)
            rope = new_rope_ref[request, step : step + 1, :].astype(jnp.float32)
            score = jnp.sum(query_lat * key, axis=1, keepdims=True)
            score = score + jnp.sum(query_rope * rope, axis=1, keepdims=True)
            fresh.append((score * SCALE, key))
        later = jnp.where(first_step, NEG, fresh[1][0])
        fresh[1] = (later, fresh[1][1])
        sums = [
            m[:, 3 * request : 3 * request + 1]
            + m[:, 3 * request + 1 : 3 * request + 2]
            + m[:, 3 * request + 2 : 3 * request + 3]
            for m in meta
        ]
        top = functools.reduce(jnp.maximum, sums + [s for s, _ in fresh])
        total = jnp.zeros((ROWS, 1), jnp.float32)
        acc = jnp.zeros((ROWS, 512), jnp.float32)
        for p, s in zip(parts, sums):
            weight = jnp.exp(s - top)
            total = total + weight
            acc = acc + weight * p[rows, :].astype(jnp.float32)
        for score, key in fresh:
            weight = jnp.exp(score - top)
            total = total + weight
            acc = acc + weight.astype(jnp.bfloat16).astype(jnp.float32) * key
        out_ref[request] = (acc / total).astype(jnp.bfloat16)


def page_table(row, pair, a, x, c, y):
    slot = jnp.arange(SLOTS, dtype=jnp.int32)
    owner_pair, a_from = slot // (2 * NX * NC), slot // (NX * NC) % 2
    x_from, c_from = slot // NC % NX, slot % NC
    y_from = serving_y(owner_pair, pair, c_from)
    holder = ((2 * pair + a_from) * NX + x_from) * NC + c_from
    place = row[y_from * SLOTS + holder]
    rope_slot = ((a_from ^ a) * 2 + (c_from ^ c)) * (NY * NX)
    rope_slot = rope_slot + (y - y_from) % NY * NX + (x - x_from) % NX
    request = place // 128
    length = jnp.where(
        request == 0, row[256] * 128 + row[258], row[257] * 128 + row[259]
    )
    valid = jnp.clip(length - (place % 128) * PAGE, 0, PAGE)
    key = jnp.where(valid > 0, request, 2)
    before = (key[None, :] < key[:, None]) | (
        (key[None, :] == key[:, None]) & (slot[None, :] < slot[:, None])
    )
    rank = jnp.sum(before.astype(jnp.int32), axis=1)
    hit = rank[:, None] == slot[None, :]
    order, rope_order, valid = (
        jnp.sum(jnp.where(hit, v[:, None], 0), axis=0) for v in (slot, rope_slot, valid)
    )
    count = jnp.stack([jnp.sum((key == r).astype(jnp.int32)) for r in range(2)])
    return order, rope_order, valid, count


def pick(array, index, axis):
    return lax.dynamic_index_in_dim(array, index, axis, keepdims=False)


def move_ropes(ropes, pair, a, x, c, y):
    ropes = ropes.reshape(PAIRS, 2, NX, NC, PAGE // 2, 2 * ROPE)
    came = []
    for s in range(NX):
        part = pick(ropes, (x + s) % NX, 2)
        if s:
            pairs = [
                (device_id(z, i, k, 0) // NY, device_id(z, (i + s) % NX, k, 0) // NY)
                for z, i, k, _ in devices()[::NY]
            ]
            part = lax.ppermute(part, "req", pairs)
        came.append(part)
    ropes = jnp.stack(came)
    came = []
    for t in range(NY):
        part = jnp.stack(
            [
                pick(ropes[:, :, :, k], served_pair(pair, (y + t) % NY, k), 1)
                for k in range(NC)
            ]
        )
        if t:
            part = lax.ppermute(part, "head", [(i, (i + t) % NY) for i in range(NY)])
        came.append(part)
    ropes = jnp.stack(came)
    came = []
    for da in range(2):
        for dc in range(2):
            part = pick(pick(ropes, c ^ dc, 1), a ^ da, 2)
            if da or dc:
                pairs = [
                    (device_id(z, i, k, 0) // NY, device_id(z ^ da, i, k ^ dc, 0) // NY)
                    for z, i, k, _ in devices()[::NY]
                ]
                part = lax.ppermute(part, "req", pairs)
            came.append(part)
    return jnp.concatenate(came).reshape(SLOTS, PAGE // 2, 2 * ROPE)


def on_device(
    latent_pages, rope_pages, page_place, lengths, q_latent, q_rope, new_latent, new_rope
):
    here = lax.axis_index("req")
    y = lax.axis_index("head")
    pair, a = here // (2 * NX * NC), here // (NX * NC) % 2
    x, c = here // NC % NX, here % NC
    lat = lax.all_to_all(
        latent_pages, AXES, 0, 0, axis_index_groups=page_groups(), tiled=True
    )
    place = page_place.astype(jnp.bfloat16)
    length = jnp.concatenate([lengths // 128, lengths % 128]).astype(jnp.bfloat16)
    row = jnp.concatenate([place, length, jnp.zeros((512 - 260,), jnp.bfloat16)])
    query_lat = q_latent.reshape(2 * ROWS, 512)
    query_rope = q_rope.reshape(2 * ROWS, ROPE)
    query = jnp.concatenate([query_lat, query_rope.reshape(META, 512)], axis=0)
    first = jnp.concatenate(
        [query, row[None, :], jnp.zeros((META - 1, 512), jnp.bfloat16)], axis=0
    )
    came = [
        lax.ppermute(query if d else first, AXES, [(t, s) for s, t in home_pairs(d)])
        for d in range(4)
    ]
    queries = []
    for part in came:
        part_rope = part[2 * ROWS : 2 * ROWS + META].reshape(2, ROWS, ROPE)
        part_lat = part[: 2 * ROWS].reshape(2, ROWS, 512)
        queries.append(jnp.concatenate([part_lat, part_rope, part_rope], axis=2))
    queries = jnp.concatenate(queries, axis=1)
    table = page_table(came[0][2 * ROWS + META].astype(jnp.int32), pair, a, x, c, y)
    rope = move_ropes(rope_pages, pair, a, x, c, y)
    whole = pl.BlockSpec(memory_space=pltpu.VMEM)
    scalars = pl.BlockSpec(memory_space=pltpu.SMEM)
    partial = jax.ShapeDtypeStruct((2 * ROWS + META, 512), jnp.bfloat16)
    parts = pl.pallas_call(
        attend_kernel,
        out_shape=[partial] * 4,
        in_specs=[scalars] * 4 + [pl.BlockSpec(memory_space=pl.ANY), whole, whole],
        out_specs=[whole] * 4,
        scratch_shapes=[
            pltpu.VMEM((SLOTS, PAGE, 512), jnp.bfloat16),
            pltpu.VMEM((SLOTS // BLOCK, 4 * ROWS, TOKENS), jnp.float32),
            pltpu.VMEM((4 * ROWS, 512), jnp.float32),
            pltpu.SemaphoreType.DMA((SLOTS,)),
        ],
        compiler_params=pltpu.CompilerParams(vmem_limit_bytes=48 * 1024 * 1024),
        cost_estimate=pl.CostEstimate(
            flops=4 * ROWS * 6144 * 1152 * 2, bytes_accessed=8 << 20, transcendentals=1 << 20
        ),
        name="attend",
    )(*table, lat, rope, queries)
    home = [lax.ppermute(part, AXES, home_pairs(d)) for d, part in enumerate(parts)]
    out = pl.pallas_call(
        merge_kernel,
        out_shape=jax.ShapeDtypeStruct((2, ROWS, 512), jnp.bfloat16),
        in_specs=[whole] * 8,
        out_specs=whole,
        name="merge",
    )(*home, query_lat, query_rope, new_latent, new_rope)
    return out.reshape(q_latent.shape)


def solution(mesh):
    return jax.shard_map(
        on_device,
        mesh=mesh,
        in_specs=(
            P(("req", "head"), None, None),
            P(("req", "head"), None),
            P("req"),
            P("req"),
            P("req", None, "head", None),
            P("req", None, "head", None),
            P("req", None, None),
            P("req", None, None),
        ),
        out_specs=P("req", None, "head", None),
        check_vma=False,
    )
```

```python
import functools
import math

import jax
import jax.numpy as jnp
from jax import lax
from jax.experimental import pallas as pl
from jax.experimental.pallas import tpu as pltpu
from jax.sharding import PartitionSpec as P

ROPE = 64
NOPE = 128
SCALE = float(NOPE + ROPE) ** -0.5 * math.log2(math.e)
NEG = -1e30

NZ, NX, NC, NY = 8, 4, 2, 4
AXES = ("req", "head")
PAIRS = NZ // 2
SLOTS = NZ * NX * NC
PAGE = 96
BLOCK = 8
TOKENS = BLOCK * PAGE
ROWS = 64
META = 16


def device_id(z, x, core, y):
    return ((z * NX + x) * NC + core) * NY + y


def served_pair(pair, y, core):
    return (pair + (1 - 2 * core) * (y + 2 * (pair % 2))) % PAIRS


def serving_y(owner_pair, pair, core):
    return ((1 - 2 * core) * (owner_pair - pair) - 2 * (pair % 2)) % NY


def page_groups():
    return [
        [
            device_id(2 * j + zo % 2, x, c, serving_y(zo // 2, j, c))
            for zo in range(NZ)
            for x in range(NX)
            for c in range(NC)
        ]
        for j in range(PAIRS)
    ]


def home_pairs(d):
    return [
        (
            device_id(z, x, c, y),
            device_id(2 * served_pair(z // 2, y, c) + z % 2, x, c, (y + d) % NY),
        )
        for z in range(NZ)
        for x in range(NX)
        for c in range(NC)
        for y in range(NY)
    ]


def contract(left, right):
    return lax.dot_general(
        left, right, (((1,), (1,)), ((), ())), preferred_element_type=jnp.float32
    )


def spread_kernel(rope_ref, out_ref):
    pages = 4
    token = lax.broadcasted_iota(jnp.int32, (pages * PAGE, pages * PAGE // 2), 0)
    pair = lax.broadcasted_iota(jnp.int32, (pages * PAGE, pages * PAGE // 2), 1)
    spread = (token // 2 == pair).astype(jnp.bfloat16)
    half = (
        lax.broadcasted_iota(jnp.int32, (pages * PAGE, 2 * ROPE), 0) % 2
        == lax.broadcasted_iota(jnp.int32, (pages * PAGE, 2 * ROPE), 1) // ROPE
    )

    def step(i, carry):
        pairs = jnp.concatenate([rope_ref[i * pages + k] for k in range(pages)], axis=0)
        keys = jnp.dot(spread, pairs, preferred_element_type=jnp.float32)
        keys = jnp.where(half, keys, 0.0).astype(jnp.bfloat16)
        for k in range(pages):
            out_ref[i * pages + k] = keys[k * PAGE : (k + 1) * PAGE, :]
        return carry

    lax.fori_loop(0, SLOTS // pages, step, 0)


def attend_kernel(
    order_ref, valid_ref, count_ref, lat_ref, keys_ref, query_ref,
    o0, o1, o2, o3, page_ref, score_ref, acc_ref, sems
):
    outs = (o0, o1, o2, o3)

    def copy(place):
        return pltpu.make_async_copy(
            lat_ref.at[order_ref[place]], page_ref.at[place], sems.at[place]
        )

    def begin(place, carry):
        copy(place).start()
        return carry

    lax.fori_loop(0, count_ref[0] + count_ref[1], begin, 0)
    lane = lax.broadcasted_iota(jnp.int32, (1, TOKENS), 1)
    meta_lane = lax.broadcasted_iota(jnp.int32, (4 * ROWS, 128), 1)
    meta = jnp.zeros((4 * ROWS, 128), jnp.float32)
    for request in range(2):
        rows = slice(request * ROWS, (request + 1) * ROWS)
        start = count_ref[0] * request
        count = count_ref[request]
        blocks = (count + BLOCK - 1) // BLOCK

        def place_of(block, index):
            return start + jnp.minimum(block * BLOCK + index, count - 1)

        def latents(block):
            return jnp.concatenate([page_ref[place_of(block, i)] for i in range(BLOCK)], axis=0)

        def score_block(block, maxima):
            for i in range(BLOCK):

                @pl.when(block * BLOCK + i < count)
                def _():
                    copy(start + block * BLOCK + i).wait()

            rope_keys = jnp.concatenate(
                [keys_ref[order_ref[place_of(block, i)]] for i in range(BLOCK)], axis=0
            )
            keys = jnp.concatenate([latents(block), rope_keys], axis=1)
            limit = jnp.zeros((1, TOKENS), jnp.int32)
            for i in range(BLOCK):
                valid = jnp.where(block * BLOCK + i < count, valid_ref[place_of(block, i)], 0)
                limit = jnp.where(lane >= i * PAGE, i * PAGE + valid, limit)
            score = contract(query_ref[request], keys) * SCALE + jnp.where(lane < limit, 0.0, NEG)
            score_ref[block] = score
            for i in range(TOKENS // 128):
                maxima = jnp.maximum(maxima, score[:, i * 128 : (i + 1) * 128])
            return maxima

        maxima = lax.fori_loop(
            0, blocks, score_block, jnp.full((4 * ROWS, 128), NEG, jnp.float32)
        )
        top = jnp.max(maxima, axis=1, keepdims=True)
        acc_ref[...] = jnp.zeros_like(acc_ref)

        def weigh_block(block, total):
            weight = jnp.exp2(score_ref[block] - top)
            for i in range(TOKENS // 128):
                total = total + weight[:, i * 128 : (i + 1) * 128]
            acc_ref[...] += jnp.dot(
                weight.astype(jnp.bfloat16), latents(block), preferred_element_type=jnp.float32
            )
            return total

        total = lax.fori_loop(
            0, blocks, weigh_block, jnp.zeros((4 * ROWS, 128), jnp.float32)
        )
        total = jnp.sum(total, axis=1, keepdims=True)
        total = jnp.where(total > 0.0, total, 1.0)
        result = (acc_ref[...] / total).astype(jnp.bfloat16)
        for i, out in enumerate(outs):
            out[rows, :] = result[i * ROWS : (i + 1) * ROWS, :]
        rest = top + jnp.log2(total)
        for part in range(3):
            piece = rest.astype(jnp.bfloat16).astype(jnp.float32)
            meta = jnp.where(meta_lane == request * 3 + part, piece, meta)
            rest = rest - piece
    meta = meta.astype(jnp.bfloat16)
    for i, out in enumerate(outs):
        part = meta[i * ROWS : (i + 1) * ROWS, :]
        out[2 * ROWS :, :] = jnp.concatenate(
            [part[k * META : (k + 1) * META, :] for k in range(4)], axis=1
        )


def merge_kernel(p0, p1, p2, p3, fresh_ref, new_lat_ref, out_ref):
    parts = (p0, p1, p2, p3)
    meta = [
        jnp.concatenate(
            [p[2 * ROWS :, k * 128 : (k + 1) * 128] for k in range(4)], axis=0
        ).astype(jnp.float32)
        for p in parts
    ]
    for request in range(2):
        rows = slice(request * ROWS, (request + 1) * ROWS)
        sums = [
            m[:, 3 * request : 3 * request + 1]
            + m[:, 3 * request + 1 : 3 * request + 2]
            + m[:, 3 * request + 2 : 3 * request + 3]
            for m in meta
        ]
        fresh = [fresh_ref[request, :, step : step + 1] for step in range(2)]
        top = functools.reduce(jnp.maximum, sums + fresh)
        total = jnp.zeros((ROWS, 1), jnp.float32)
        acc = jnp.zeros((ROWS, 512), jnp.float32)
        for part, score in zip(parts, sums):
            weight = jnp.exp2(score - top)
            total = total + weight
            acc = acc + weight * part[rows, :].astype(jnp.float32)
        for step, score in enumerate(fresh):
            weight = jnp.exp2(score - top)
            total = total + weight
            key = new_lat_ref[request, step : step + 1, :].astype(jnp.float32)
            acc = acc + weight.astype(jnp.bfloat16).astype(jnp.float32) * key
        out_ref[request] = (acc / total).astype(jnp.bfloat16)


def fresh_scores(q_latent, q_rope, new_latent, new_rope):
    dims = (((3,), (2,)), ((0,), (0,)))
    score = lax.dot_general(q_latent, new_latent, dims, preferred_element_type=jnp.float32)
    score = score + lax.dot_general(q_rope, new_rope, dims, preferred_element_type=jnp.float32)
    step = jnp.arange(2, dtype=jnp.int32)
    seen = step[None, None, None, :] <= step[None, :, None, None]
    return jnp.where(seen, score * SCALE, NEG).reshape(2, ROWS, 2)


def page_table(row, pair):
    slot = jnp.arange(SLOTS, dtype=jnp.int32)
    owner_pair, a_from = slot // (2 * NX * NC), slot // (NX * NC) % 2
    x_from, c_from = slot // NC % NX, slot % NC
    y_from = serving_y(owner_pair, pair, c_from)
    holder = device_id(2 * pair + a_from, x_from, c_from, 0) // NY
    place = row[y_from * SLOTS + holder]
    request = place // 128
    length = jnp.where(
        request == 0, row[256] * 128 + row[258], row[257] * 128 + row[259]
    )
    valid = jnp.clip(length - (place % 128) * PAGE, 0, PAGE)
    key = jnp.where(valid > 0, request, 2)
    before = (key[None, :] < key[:, None]) | (
        (key[None, :] == key[:, None]) & (slot[None, :] < slot[:, None])
    )
    rank = jnp.sum(before.astype(jnp.int32), axis=1)
    hit = rank[:, None] == slot[None, :]
    order, valid = (jnp.sum(jnp.where(hit, v[:, None], 0), axis=0) for v in (slot, valid))
    count = jnp.stack([jnp.sum((key == r).astype(jnp.int32)) for r in range(2)])
    return order, valid, count


def on_device(
    latent_pages, rope_pages, page_place, lengths, q_latent, q_rope, new_latent, new_rope
):
    here = lax.axis_index("req")
    pair = here // (2 * NX * NC)
    place = page_place.astype(jnp.bfloat16)
    length = jnp.concatenate([lengths // 128, lengths % 128]).astype(jnp.bfloat16)
    row = jnp.pad(jnp.concatenate([place, length]), (0, 512 - 260))
    row = jnp.broadcast_to(row[None, :], (META, 512))
    query = jnp.concatenate(
        [q_latent.reshape(2 * ROWS, 512), q_rope.reshape(META, 512)], axis=0
    )
    first = jnp.concatenate([query, row], axis=0)
    came = [
        lax.ppermute(query if d else first, AXES, [(t, s) for s, t in home_pairs(d)])
        for d in range(4)
    ]
    whole = pl.BlockSpec(memory_space=pltpu.VMEM)
    scalars = pl.BlockSpec(memory_space=pltpu.SMEM)
    exchange = functools.partial(
        lax.all_to_all,
        axis_name=AXES,
        split_axis=0,
        concat_axis=0,
        axis_index_groups=page_groups(),
        tiled=True,
    )
    rope = exchange(rope_pages.reshape(SLOTS, PAGE // 2, 2 * ROPE))
    latent_pages, rope, came = lax.optimization_barrier((latent_pages, rope, came))
    lat = exchange(latent_pages)
    queries = []
    for part in came:
        part_rope = part[2 * ROWS : 2 * ROWS + META].reshape(2, ROWS, ROPE)
        part_lat = part[: 2 * ROWS].reshape(2, ROWS, 512)
        queries.append(jnp.concatenate([part_lat, part_rope, part_rope], axis=2))
    queries = jnp.concatenate(queries, axis=1)
    keys = pl.pallas_call(
        spread_kernel,
        out_shape=jax.ShapeDtypeStruct((SLOTS, PAGE, 2 * ROPE), jnp.bfloat16),
        in_specs=[whole],
        out_specs=whole,
        name="spread",
    )(rope)
    table = page_table(came[0][2 * ROWS + META].astype(jnp.int32), pair)
    partial = jax.ShapeDtypeStruct((2 * ROWS + META, 512), jnp.bfloat16)
    parts = pl.pallas_call(
        attend_kernel,
        out_shape=[partial] * 4,
        in_specs=[scalars] * 3 + [pl.BlockSpec(memory_space=pl.ANY), whole, whole],
        out_specs=[whole] * 4,
        scratch_shapes=[
            pltpu.VMEM((SLOTS, PAGE, 512), jnp.bfloat16),
            pltpu.VMEM((SLOTS // BLOCK, 4 * ROWS, TOKENS), jnp.float32),
            pltpu.VMEM((4 * ROWS, 512), jnp.float32),
            pltpu.SemaphoreType.DMA((SLOTS,)),
        ],
        compiler_params=pltpu.CompilerParams(vmem_limit_bytes=20 * 1024 * 1024),
        cost_estimate=pl.CostEstimate(
            flops=4 * ROWS * 6144 * 1152 * 2, bytes_accessed=8 << 20, transcendentals=1 << 20
        ),
        name="attend",
    )(*table, lat, keys, queries)
    home = [lax.ppermute(part, AXES, home_pairs(d)) for d, part in enumerate(parts)]
    out = pl.pallas_call(
        merge_kernel,
        out_shape=jax.ShapeDtypeStruct((2, ROWS, 512), jnp.bfloat16),
        in_specs=[whole] * 6,
        out_specs=whole,
        name="merge",
    )(*home, fresh_scores(q_latent, q_rope, new_latent, new_rope), new_latent)
    return out.reshape(q_latent.shape)


def solution(mesh):
    return jax.shard_map(
        on_device,
        mesh=mesh,
        in_specs=(
            P(("req", "head"), None, None),
            P(("req", "head"), None),
            P("req"),
            P("req"),
            P("req", None, "head", None),
            P("req", None, "head", None),
            P("req", None, None),
            P("req", None, None),
        ),
        out_specs=P("req", None, "head", None),
        check_vma=False,
    )
```

```python
import functools
import math

import jax
import jax.numpy as jnp
from jax import lax
from jax.experimental import pallas as pl
from jax.experimental.pallas import tpu as pltpu
from jax.sharding import PartitionSpec as P

ROPE = 64
NOPE = 128
SCALE = float(NOPE + ROPE) ** -0.5 * math.log2(math.e)
NEG = -1e30

NZ, NX, NC, NY = 8, 4, 2, 4
AXES = ("req", "head")
PAIRS = NZ // 2
SLOTS = NZ * NX * NC
PAGE = 96
BLOCK = 8
TOKENS = BLOCK * PAGE
ROWS = 64
META = 16


def device_id(z, x, core, y):
    return ((z * NX + x) * NC + core) * NY + y


def served_pair(pair, y, core):
    return (pair + (1 - 2 * core) * (y + 2 * (pair % 2))) % PAIRS


def serving_y(owner_pair, pair, core):
    return ((1 - 2 * core) * (owner_pair - pair) - 2 * (pair % 2)) % NY


def page_groups():
    return [
        [
            device_id(2 * j + zo % 2, x, c, serving_y(zo // 2, j, c))
            for zo in range(NZ)
            for x in range(NX)
            for c in range(NC)
        ]
        for j in range(PAIRS)
    ]


def home_pairs(d):
    return [
        (
            device_id(z, x, c, y),
            device_id(2 * served_pair(z // 2, y, c) + z % 2, x, c, (y + d) % NY),
        )
        for z in range(NZ)
        for x in range(NX)
        for c in range(NC)
        for y in range(NY)
    ]


def contract(left, right):
    return lax.dot_general(
        left, right, (((1,), (1,)), ((), ())), preferred_element_type=jnp.float32
    )


def spread_kernel(rope_ref, out_ref):
    pages = 4
    token = lax.broadcasted_iota(jnp.int32, (pages * PAGE, pages * PAGE // 2), 0)
    pair = lax.broadcasted_iota(jnp.int32, (pages * PAGE, pages * PAGE // 2), 1)
    spread = (token // 2 == pair).astype(jnp.bfloat16)
    half = (
        lax.broadcasted_iota(jnp.int32, (pages * PAGE, 2 * ROPE), 0) % 2
        == lax.broadcasted_iota(jnp.int32, (pages * PAGE, 2 * ROPE), 1) // ROPE
    )

    def step(i, carry):
        pairs = jnp.concatenate([rope_ref[i * pages + k] for k in range(pages)], axis=0)
        keys = jnp.dot(spread, pairs, preferred_element_type=jnp.float32)
        keys = jnp.where(half, keys, 0.0).astype(jnp.bfloat16)
        for k in range(pages):
            out_ref[i * pages + k] = keys[k * PAGE : (k + 1) * PAGE, :]
        return carry

    lax.fori_loop(0, SLOTS // pages, step, 0)


def attend_kernel(
    order_ref, valid_ref, count_ref, lat_ref, keys_ref, query_ref,
    o0, o1, o2, o3, score_ref, acc_ref
):
    outs = (o0, o1, o2, o3)
    meta_lane = lax.broadcasted_iota(jnp.int32, (4 * ROWS, 128), 1)
    meta = jnp.zeros((4 * ROWS, 128), jnp.float32)
    for request in range(2):
        start = count_ref[0] * request
        count = count_ref[request]
        blocks = (count + BLOCK - 1) // BLOCK
        doubles, single = blocks // 2, blocks % 2

        def slots(block, size):
            return [
                start + jnp.minimum(block * BLOCK + i, count - 1) for i in range(size * BLOCK)
            ]

        def latents(places):
            return jnp.concatenate([lat_ref[order_ref[p]] for p in places], axis=0)

        def score_blocks(size, block, maxima):
            places = slots(block, size)
            rope_keys = jnp.concatenate([keys_ref[order_ref[p]] for p in places], axis=0)
            keys = jnp.concatenate([latents(places), rope_keys], axis=1)
            lane = lax.broadcasted_iota(jnp.int32, (1, size * TOKENS), 1)
            limit = jnp.zeros((1, size * TOKENS), jnp.int32)
            for i, p in enumerate(places):
                valid = jnp.where(block * BLOCK + i < count, valid_ref[p], 0)
                limit = jnp.where(lane >= i * PAGE, i * PAGE + valid, limit)
            score = contract(query_ref[request], keys) * SCALE
            score = score + jnp.where(lane < limit, 0.0, NEG)
            for i in range(size):
                score_ref[block + i] = score[:, i * TOKENS : (i + 1) * TOKENS]
            for i in range(size * TOKENS // 128):
                maxima = jnp.maximum(maxima, score[:, i * 128 : (i + 1) * 128])
            return maxima

        def weigh_blocks(size, block, total):
            weight = [jnp.exp2(score_ref[block + i] - top) for i in range(size)]
            for part in weight:
                for i in range(TOKENS // 128):
                    total = total + part[:, i * 128 : (i + 1) * 128]
            weight = jnp.concatenate([w.astype(jnp.bfloat16) for w in weight], axis=1)
            acc_ref[...] += jnp.dot(
                weight, latents(slots(block, size)), preferred_element_type=jnp.float32
            )
            return total

        def over(step, carry):
            carry = lax.fori_loop(0, doubles, lambda i, c: step(2, 2 * i, c), carry)
            return lax.fori_loop(0, single, lambda i, c: step(1, 2 * doubles, c), carry)

        maxima = over(score_blocks, jnp.full((4 * ROWS, 128), NEG, jnp.float32))
        top = jnp.max(maxima, axis=1, keepdims=True)
        acc_ref[...] = jnp.zeros_like(acc_ref)
        total = over(weigh_blocks, jnp.zeros((4 * ROWS, 128), jnp.float32))
        total = jnp.sum(total, axis=1, keepdims=True)
        total = jnp.where(total > 0.0, total, 1.0)
        result = (acc_ref[...] / total).astype(jnp.bfloat16)
        for i, out in enumerate(outs):
            out[request * ROWS : (request + 1) * ROWS, :] = result[i * ROWS : (i + 1) * ROWS, :]
        rest = top + jnp.log2(total)
        for part in range(3):
            piece = rest.astype(jnp.bfloat16).astype(jnp.float32)
            meta = jnp.where(meta_lane == request * 3 + part, piece, meta)
            rest = rest - piece
    meta = meta.astype(jnp.bfloat16)
    for i, out in enumerate(outs):
        part = meta[i * ROWS : (i + 1) * ROWS, :]
        out[2 * ROWS :, :] = jnp.concatenate(
            [part[k * META : (k + 1) * META, :] for k in range(4)], axis=1
        )


def merge_kernel(p0, p1, p2, p3, fresh_ref, new_lat_ref, out_ref):
    parts = (p0, p1, p2, p3)
    meta = [
        jnp.concatenate(
            [p[2 * ROWS :, k * 128 : (k + 1) * 128] for k in range(4)], axis=0
        ).astype(jnp.float32)
        for p in parts
    ]
    for request in range(2):
        rows = slice(request * ROWS, (request + 1) * ROWS)
        sums = [
            m[:, 3 * request : 3 * request + 1]
            + m[:, 3 * request + 1 : 3 * request + 2]
            + m[:, 3 * request + 2 : 3 * request + 3]
            for m in meta
        ]
        fresh = [fresh_ref[request, :, step : step + 1] for step in range(2)]
        top = functools.reduce(jnp.maximum, sums + fresh)
        total = jnp.zeros((ROWS, 1), jnp.float32)
        acc = jnp.zeros((ROWS, 512), jnp.float32)
        for part, score in zip(parts, sums):
            weight = jnp.exp2(score - top)
            total = total + weight
            acc = acc + weight * part[rows, :].astype(jnp.float32)
        for step, score in enumerate(fresh):
            weight = jnp.exp2(score - top)
            total = total + weight
            key = new_lat_ref[request, step : step + 1, :].astype(jnp.float32)
            acc = acc + weight.astype(jnp.bfloat16).astype(jnp.float32) * key
        out_ref[request] = (acc / total).astype(jnp.bfloat16)


def fresh_scores(q_latent, q_rope, new_latent, new_rope):
    dims = (((3,), (2,)), ((0,), (0,)))
    score = lax.dot_general(q_latent, new_latent, dims, preferred_element_type=jnp.float32)
    score = score + lax.dot_general(q_rope, new_rope, dims, preferred_element_type=jnp.float32)
    step = jnp.arange(2, dtype=jnp.int32)
    seen = step[None, None, None, :] <= step[None, :, None, None]
    return jnp.where(seen, score * SCALE, NEG).reshape(2, ROWS, 2)


def page_table(row, pair):
    slot = jnp.arange(SLOTS, dtype=jnp.int32)
    owner_pair, a_from = slot // (2 * NX * NC), slot // (NX * NC) % 2
    x_from, c_from = slot // NC % NX, slot % NC
    y_from = serving_y(owner_pair, pair, c_from)
    holder = device_id(2 * pair + a_from, x_from, c_from, 0) // NY
    place = row[y_from * SLOTS + holder]
    request = place // 128
    length = jnp.where(
        request == 0, row[256] * 128 + row[258], row[257] * 128 + row[259]
    )
    valid = jnp.clip(length - (place % 128) * PAGE, 0, PAGE)
    key = jnp.where(valid > 0, request, 2)
    before = (key[None, :] < key[:, None]) | (
        (key[None, :] == key[:, None]) & (slot[None, :] < slot[:, None])
    )
    rank = jnp.sum(before.astype(jnp.int32), axis=1)
    hit = rank[:, None] == slot[None, :]
    order, valid = (jnp.sum(jnp.where(hit, v[:, None], 0), axis=0) for v in (slot, valid))
    count = jnp.stack([jnp.sum((key == r).astype(jnp.int32)) for r in range(2)])
    return order, valid, count


def on_device(
    latent_pages, rope_pages, page_place, lengths, q_latent, q_rope, new_latent, new_rope
):
    here = lax.axis_index("req")
    pair = here // (2 * NX * NC)
    place = page_place.astype(jnp.bfloat16)
    length = jnp.concatenate([lengths // 128, lengths % 128]).astype(jnp.bfloat16)
    row = jnp.pad(jnp.concatenate([place, length]), (0, 512 - 260))
    row = jnp.broadcast_to(row[None, :], (META, 512))
    query = jnp.concatenate(
        [q_latent.reshape(2 * ROWS, 512), q_rope.reshape(META, 512)], axis=0
    )
    first = jnp.concatenate([query, row], axis=0)
    came = [
        lax.ppermute(query if d else first, AXES, [(t, s) for s, t in home_pairs(d)])
        for d in range(4)
    ]
    whole = pl.BlockSpec(memory_space=pltpu.VMEM)
    scalars = pl.BlockSpec(memory_space=pltpu.SMEM)
    exchange = functools.partial(
        lax.all_to_all,
        axis_name=AXES,
        split_axis=0,
        concat_axis=0,
        axis_index_groups=page_groups(),
        tiled=True,
    )
    rope = exchange(rope_pages.reshape(SLOTS, PAGE // 2, 2 * ROPE))
    latent_pages, rope, came = lax.optimization_barrier((latent_pages, rope, came))
    lat = exchange(latent_pages)
    queries = []
    for part in came:
        part_rope = part[2 * ROWS : 2 * ROWS + META].reshape(2, ROWS, ROPE)
        part_lat = part[: 2 * ROWS].reshape(2, ROWS, 512)
        queries.append(jnp.concatenate([part_lat, part_rope, part_rope], axis=2))
    queries = jnp.concatenate(queries, axis=1)
    keys = pl.pallas_call(
        spread_kernel,
        out_shape=jax.ShapeDtypeStruct((SLOTS, PAGE, 2 * ROPE), jnp.bfloat16),
        in_specs=[whole],
        out_specs=whole,
        compiler_params=pltpu.CompilerParams(vmem_limit_bytes=8 * 1024 * 1024),
        name="spread",
    )(rope)
    table = page_table(came[0][2 * ROWS + META].astype(jnp.int32), pair)
    partial = jax.ShapeDtypeStruct((2 * ROWS + META, 512), jnp.bfloat16)
    parts = pl.pallas_call(
        attend_kernel,
        out_shape=[partial] * 4,
        in_specs=[scalars] * 3 + [whole] * 3,
        out_specs=[whole] * 4,
        scratch_shapes=[
            pltpu.VMEM((SLOTS // BLOCK, 4 * ROWS, TOKENS), jnp.float32),
            pltpu.VMEM((4 * ROWS, 512), jnp.float32),
        ],
        compiler_params=pltpu.CompilerParams(vmem_limit_bytes=32 * 1024 * 1024),
        cost_estimate=pl.CostEstimate(
            flops=4 * ROWS * 6144 * 1152 * 2, bytes_accessed=8 << 20, transcendentals=1 << 20
        ),
        name="attend",
    )(*table, lat, keys, queries)
    home = [lax.ppermute(part, AXES, home_pairs(d)) for d, part in enumerate(parts)]
    out = pl.pallas_call(
        merge_kernel,
        out_shape=jax.ShapeDtypeStruct((2, ROWS, 512), jnp.bfloat16),
        in_specs=[whole] * 6,
        out_specs=whole,
        compiler_params=pltpu.CompilerParams(vmem_limit_bytes=4 * 1024 * 1024),
        name="merge",
    )(*home, fresh_scores(q_latent, q_rope, new_latent, new_rope), new_latent)
    return out.reshape(q_latent.shape)


def solution(mesh):
    return jax.shard_map(
        on_device,
        mesh=mesh,
        in_specs=(
            P(("req", "head"), None, None),
            P(("req", "head"), None),
            P("req"),
            P("req"),
            P("req", None, "head", None),
            P("req", None, "head", None),
            P("req", None, None),
            P("req", None, None),
        ),
        out_specs=P("req", None, "head", None),
        check_vma=False,
    )
```

```python
import functools
import math

import jax
import jax.numpy as jnp
from jax import lax
from jax.experimental import pallas as pl
from jax.experimental.pallas import tpu as pltpu
from jax.sharding import PartitionSpec as P

ROPE = 64
NOPE = 128
SCALE = float(NOPE + ROPE) ** -0.5 * math.log2(math.e)
NEG = -1e30

NZ, NX, NC, NY = 8, 4, 2, 4
AXES = ("req", "head")
PAIRS = NZ // 2
SLOTS = NZ * NX * NC
PAGE = 96
BLOCK = 8
SPREAD = 4
TOKENS = BLOCK * PAGE
ROWS = 64
META = 16
QCOST = 10**11


def device_id(z, x, core, y):
    return ((z * NX + x) * NC + core) * NY + y


def served_pair(pair, y, core):
    return (pair + (1 - 2 * core) * (y + 2 * (pair % 2))) % PAIRS


def serving_y(owner_pair, pair, core):
    return ((1 - 2 * core) * (owner_pair - pair) - 2 * (pair % 2)) % NY


def page_groups():
    return [
        [
            device_id(2 * j + zo % 2, x, c, serving_y(zo // 2, j, c))
            for zo in range(NZ)
            for x in range(NX)
            for c in range(NC)
        ]
        for j in range(PAIRS)
    ]


def home_pairs(d):
    return [
        (
            device_id(z, x, c, y),
            device_id(2 * served_pair(z // 2, y, c) + z % 2, x, c, (y + d) % NY),
        )
        for z in range(NZ)
        for x in range(NX)
        for c in range(NC)
        for y in range(NY)
    ]


def contract(left, right):
    return lax.dot_general(
        left, right, (((1,), (1,)), ((), ())), preferred_element_type=jnp.float32
    )


def query_kernel(q0, q1, q2, q3, out_ref):
    for request in range(2):
        for i, query in enumerate((q0, q1, q2, q3)):
            rows = slice(i * ROWS, (i + 1) * ROWS)
            out_ref[request, rows, :512] = query[request * ROWS : (request + 1) * ROWS, :]
            for k in range(2):
                rows = slice(i * ROWS + k * 32, i * ROWS + (k + 1) * 32)
                tile = slice((2 * request + k) * 128, (2 * request + k + 1) * 128)
                out_ref[request, rows, 512:] = query[2 * ROWS : 2 * ROWS + 32, tile]


def attend_kernel(
    order_ref, valid_ref, count_ref, lat_ref, rope_ref, query_ref,
    o0, o1, o2, o3, score_ref, acc_ref
):
    outs = (o0, o1, o2, o3)
    token = lax.broadcasted_iota(jnp.int32, (SPREAD * PAGE, SPREAD * PAGE // 2), 0)
    pair = lax.broadcasted_iota(jnp.int32, (SPREAD * PAGE, SPREAD * PAGE // 2), 1)
    spread = (token // 2 == pair).astype(jnp.bfloat16)
    half = (
        lax.broadcasted_iota(jnp.int32, (SPREAD * PAGE, 2 * ROPE), 0) % 2
        == lax.broadcasted_iota(jnp.int32, (SPREAD * PAGE, 2 * ROPE), 1) // ROPE
    )

    def rope_keys(places):
        pairs = jnp.concatenate([rope_ref[order_ref[p]] for p in places], axis=0)
        keys = jnp.dot(spread, pairs, preferred_element_type=jnp.float32)
        return jnp.where(half, keys, 0.0).astype(jnp.bfloat16)

    meta_lane = lax.broadcasted_iota(jnp.int32, (4 * ROWS, 128), 1)
    meta = jnp.zeros((4 * ROWS, 128), jnp.float32)
    for request in range(2):
        start = count_ref[0] * request
        count = count_ref[request]
        blocks = (count + BLOCK - 1) // BLOCK
        doubles, single = blocks // 2, blocks % 2

        def slots(block, size):
            return [
                start + jnp.minimum(block * BLOCK + i, count - 1) for i in range(size * BLOCK)
            ]

        def latents(places):
            return jnp.concatenate([lat_ref[order_ref[p]] for p in places], axis=0)

        def score_blocks(size, block, maxima):
            places = slots(block, size)
            ropes = [rope_keys(places[i : i + SPREAD]) for i in range(0, len(places), SPREAD)]
            keys = jnp.concatenate([latents(places), jnp.concatenate(ropes, axis=0)], axis=1)
            lane = lax.broadcasted_iota(jnp.int32, (1, size * TOKENS), 1)
            limit = jnp.zeros((1, size * TOKENS), jnp.int32)
            for i, p in enumerate(places):
                valid = jnp.where(block * BLOCK + i < count, valid_ref[p], 0)
                limit = jnp.where(lane >= i * PAGE, i * PAGE + valid, limit)
            score = contract(query_ref[request], keys) * SCALE
            score = score + jnp.where(lane < limit, 0.0, NEG)
            for i in range(size):
                score_ref[block + i] = score[:, i * TOKENS : (i + 1) * TOKENS]
            for i in range(size * TOKENS // 128):
                maxima = jnp.maximum(maxima, score[:, i * 128 : (i + 1) * 128])
            return maxima

        def weigh_blocks(size, block, total):
            weight = [jnp.exp2(score_ref[block + i] - top) for i in range(size)]
            for part in weight:
                for i in range(TOKENS // 128):
                    total = total + part[:, i * 128 : (i + 1) * 128]
            weight = jnp.concatenate([w.astype(jnp.bfloat16) for w in weight], axis=1)
            acc_ref[...] += jnp.dot(
                weight, latents(slots(block, size)), preferred_element_type=jnp.float32
            )
            return total

        def over(step, carry):
            carry = lax.fori_loop(0, doubles, lambda i, c: step(2, 2 * i, c), carry)
            return lax.fori_loop(0, single, lambda i, c: step(1, 2 * doubles, c), carry)

        maxima = over(score_blocks, jnp.full((4 * ROWS, 128), NEG, jnp.float32))
        top = jnp.max(maxima, axis=1, keepdims=True)
        acc_ref[...] = jnp.zeros_like(acc_ref)
        total = over(weigh_blocks, jnp.zeros((4 * ROWS, 128), jnp.float32))
        total = jnp.sum(total, axis=1, keepdims=True)
        total = jnp.where(total > 0.0, total, 1.0)
        result = (acc_ref[...] / total).astype(jnp.bfloat16)
        for i, out in enumerate(outs):
            out[request * ROWS : (request + 1) * ROWS, :] = result[i * ROWS : (i + 1) * ROWS, :]
        rest = top + jnp.log2(total)
        for part in range(3):
            piece = rest.astype(jnp.bfloat16).astype(jnp.float32)
            meta = jnp.where(meta_lane == request * 3 + part, piece, meta)
            rest = rest - piece
    meta = meta.astype(jnp.bfloat16)
    for i, out in enumerate(outs):
        part = meta[i * ROWS : (i + 1) * ROWS, :]
        out[2 * ROWS :, :] = jnp.concatenate(
            [part[k * META : (k + 1) * META, :] for k in range(4)], axis=1
        )


def merge_kernel(p0, p1, p2, p3, fresh_ref, new_lat_ref, out_ref):
    parts = (p0, p1, p2, p3)
    meta = [
        jnp.concatenate(
            [p[2 * ROWS :, k * 128 : (k + 1) * 128] for k in range(4)], axis=0
        ).astype(jnp.float32)
        for p in parts
    ]
    for request in range(2):
        rows = slice(request * ROWS, (request + 1) * ROWS)
        sums = [
            m[:, 3 * request : 3 * request + 1]
            + m[:, 3 * request + 1 : 3 * request + 2]
            + m[:, 3 * request + 2 : 3 * request + 3]
            for m in meta
        ]
        fresh = [fresh_ref[request, :, step : step + 1] for step in range(2)]
        top = functools.reduce(jnp.maximum, sums + fresh)
        total = jnp.zeros((ROWS, 1), jnp.float32)
        acc = jnp.zeros((ROWS, 512), jnp.float32)
        for part, score in zip(parts, sums):
            weight = jnp.exp2(score - top)
            total = total + weight
            acc = acc + weight * part[rows, :].astype(jnp.float32)
        for step, score in enumerate(fresh):
            weight = jnp.exp2(score - top)
            total = total + weight
            key = new_lat_ref[request, step : step + 1, :].astype(jnp.float32)
            acc = acc + weight.astype(jnp.bfloat16).astype(jnp.float32) * key
        out_ref[request] = (acc / total).astype(jnp.bfloat16)


def fresh_scores(q_latent, q_rope, new_latent, new_rope):
    dims = (((3,), (2,)), ((0,), (0,)))
    score = lax.dot_general(q_latent, new_latent, dims, preferred_element_type=jnp.float32)
    score = score + lax.dot_general(q_rope, new_rope, dims, preferred_element_type=jnp.float32)
    step = jnp.arange(2, dtype=jnp.int32)
    seen = step[None, None, None, :] <= step[None, :, None, None]
    return jnp.where(seen, score * SCALE, NEG).reshape(2, ROWS, 2)


def page_table(row, pair):
    slot = jnp.arange(SLOTS, dtype=jnp.int32)
    owner_pair, a_from = slot // (2 * NX * NC), slot // (NX * NC) % 2
    x_from, c_from = slot // NC % NX, slot % NC
    y_from = serving_y(owner_pair, pair, c_from)
    holder = device_id(2 * pair + a_from, x_from, c_from, 0) // NY
    place = row[y_from * SLOTS + holder]
    request = place // 128
    length = jnp.where(
        request == 0, row[256] * 128 + row[258], row[257] * 128 + row[259]
    )
    valid = jnp.clip(length - (place % 128) * PAGE, 0, PAGE)
    key = jnp.where(valid > 0, request, 2)
    before = (key[None, :] < key[:, None]) | (
        (key[None, :] == key[:, None]) & (slot[None, :] < slot[:, None])
    )
    rank = jnp.sum(before.astype(jnp.int32), axis=1)
    hit = rank[:, None] == slot[None, :]
    order, valid = (jnp.sum(jnp.where(hit, v[:, None], 0), axis=0) for v in (slot, valid))
    count = jnp.stack([jnp.sum((key == r).astype(jnp.int32)) for r in range(2)])
    return order, valid, count


def on_device(
    latent_pages, rope_pages, page_place, lengths, q_latent, q_rope, new_latent, new_rope
):
    here = lax.axis_index("req")
    pair = here // (2 * NX * NC)
    place = page_place.astype(jnp.bfloat16)
    length = jnp.concatenate([lengths // 128, lengths % 128]).astype(jnp.bfloat16)
    row = jnp.pad(jnp.concatenate([place, length]), (0, 512 - 260))
    row = jnp.broadcast_to(row[None, :], (META, 512))
    query_rope = q_rope.reshape(2 * ROWS, ROPE)
    twice = jnp.concatenate([query_rope, query_rope], axis=1).reshape(4, 32, 2 * ROPE)
    twice = jnp.concatenate([twice[k] for k in range(4)], axis=1)
    query = jnp.concatenate([q_latent.reshape(2 * ROWS, 512), twice], axis=0)
    first = jnp.concatenate([query, row], axis=0)
    came = [
        lax.ppermute(query if d else first, AXES, [(t, s) for s, t in home_pairs(d)])
        for d in range(4)
    ]
    whole = pl.BlockSpec(memory_space=pltpu.VMEM)
    scalars = pl.BlockSpec(memory_space=pltpu.SMEM)
    exchange = functools.partial(
        lax.all_to_all,
        axis_name=AXES,
        split_axis=0,
        concat_axis=0,
        axis_index_groups=page_groups(),
        tiled=True,
    )
    lat = exchange(latent_pages)
    ropes = rope_pages.reshape(SLOTS, PAGE // 2, 2 * ROPE)
    lat, ropes = lax.optimization_barrier((lat, ropes))
    rope = exchange(ropes)
    queries = pl.pallas_call(
        query_kernel,
        out_shape=jax.ShapeDtypeStruct((2, 4 * ROWS, 512 + 2 * ROPE), jnp.bfloat16),
        in_specs=[whole] * 4,
        out_specs=whole,
        cost_estimate=pl.CostEstimate(flops=QCOST, bytes_accessed=2 << 20, transcendentals=0),
        compiler_params=pltpu.CompilerParams(vmem_limit_bytes=8 * 1024 * 1024),
        name="queries",
    )(*came)
    table = page_table(came[0][2 * ROWS + 32].astype(jnp.int32), pair)
    partial = jax.ShapeDtypeStruct((2 * ROWS + META, 512), jnp.bfloat16)
    parts = pl.pallas_call(
        attend_kernel,
        out_shape=[partial] * 4,
        in_specs=[scalars] * 3 + [whole] * 3,
        out_specs=[whole] * 4,
        scratch_shapes=[
            pltpu.VMEM((SLOTS // BLOCK, 4 * ROWS, TOKENS), jnp.float32),
            pltpu.VMEM((4 * ROWS, 512), jnp.float32),
        ],
        compiler_params=pltpu.CompilerParams(vmem_limit_bytes=18 * 1024 * 1024),
        cost_estimate=pl.CostEstimate(
            flops=4 * ROWS * 6144 * 1152 * 2, bytes_accessed=8 << 20, transcendentals=1 << 20
        ),
        name="attend",
    )(*table, lat, rope, queries)
    home = [lax.ppermute(part, AXES, home_pairs(d)) for d, part in enumerate(parts)]
    out = pl.pallas_call(
        merge_kernel,
        out_shape=jax.ShapeDtypeStruct((2, ROWS, 512), jnp.bfloat16),
        in_specs=[whole] * 6,
        out_specs=whole,
        compiler_params=pltpu.CompilerParams(vmem_limit_bytes=4 * 1024 * 1024),
        name="merge",
    )(*home, fresh_scores(q_latent, q_rope, new_latent, new_rope), new_latent)
    return out.reshape(q_latent.shape)


def solution(mesh):
    return jax.shard_map(
        on_device,
        mesh=mesh,
        in_specs=(
            P(("req", "head"), None, None),
            P(("req", "head"), None),
            P("req"),
            P("req"),
            P("req", None, "head", None),
            P("req", None, "head", None),
            P("req", None, None),
            P("req", None, None),
        ),
        out_specs=P("req", None, "head", None),
        check_vma=False,
    )
```

```python
import functools
import math

import jax
import jax.numpy as jnp
from jax import lax
from jax.experimental import pallas as pl
from jax.experimental.pallas import tpu as pltpu
from jax.sharding import PartitionSpec as P

ROPE = 64
NOPE = 128
SCALE = float(NOPE + ROPE) ** -0.5 * math.log2(math.e)
NEG = -1e30

NZ, NX, NC, NY = 8, 4, 2, 4
AXES = ("req", "head")
PAIRS = NZ // 2
SLOTS = NZ * NX * NC
PAGE = 96
BLOCK = 8
SPREAD = 4
TOKENS = BLOCK * PAGE
ROWS = 64
META = 16
QCOST = 10**11


def device_id(z, x, core, y):
    return ((z * NX + x) * NC + core) * NY + y


def served_pair(pair, y, core):
    return (pair + (1 - 2 * core) * (y + 2 * (pair % 2))) % PAIRS


def serving_y(owner_pair, pair, core):
    return ((1 - 2 * core) * (owner_pair - pair) - 2 * (pair % 2)) % NY


def page_groups():
    return [
        [
            device_id(2 * j + zo % 2, x, c, serving_y(zo // 2, j, c))
            for zo in range(NZ)
            for x in range(NX)
            for c in range(NC)
        ]
        for j in range(PAIRS)
    ]


def home_pairs(d):
    return [
        (
            device_id(z, x, c, y),
            device_id(2 * served_pair(z // 2, y, c) + z % 2, x, c, (y + d) % NY),
        )
        for z in range(NZ)
        for x in range(NX)
        for c in range(NC)
        for y in range(NY)
    ]


def contract(left, right):
    return lax.dot_general(
        left, right, (((1,), (1,)), ((), ())), preferred_element_type=jnp.float32
    )


def query_kernel(q0, q1, q2, q3, out_ref):
    first = lax.broadcasted_iota(jnp.int32, (META, 2 * ROPE), 1) < ROPE
    for request in range(2):
        for i, query in enumerate((q0, q1, q2, q3)):
            rows = slice(i * ROWS, (i + 1) * ROWS)
            out_ref[request, rows, :512] = query[request * ROWS : (request + 1) * ROWS, :]
            for k in range(2):
                tile = slice((2 * request + k) * 128, (2 * request + k + 1) * 128)
                both = query[2 * ROWS : 2 * ROWS + META, tile].astype(jnp.float32)
                swapped = pltpu.roll(both, ROPE, 1)
                pair = (jnp.where(first, both, swapped), jnp.where(first, swapped, both))
                for h, part in enumerate(pair):
                    row = i * ROWS + k * 32 + h * META
                    out_ref[request, row : row + META, 512:] = part.astype(jnp.bfloat16)


def attend_kernel(
    order_ref, valid_ref, count_ref, lat_ref, rope_ref, query_ref,
    o0, o1, o2, o3, score_ref, acc_ref
):
    outs = (o0, o1, o2, o3)
    token = lax.broadcasted_iota(jnp.int32, (SPREAD * PAGE, SPREAD * PAGE // 2), 0)
    pair = lax.broadcasted_iota(jnp.int32, (SPREAD * PAGE, SPREAD * PAGE // 2), 1)
    spread = (token // 2 == pair).astype(jnp.bfloat16)
    half = (
        lax.broadcasted_iota(jnp.int32, (SPREAD * PAGE, 2 * ROPE), 0) % 2
        == lax.broadcasted_iota(jnp.int32, (SPREAD * PAGE, 2 * ROPE), 1) // ROPE
    )

    def rope_keys(places):
        pairs = jnp.concatenate([rope_ref[order_ref[p]] for p in places], axis=0)
        keys = jnp.dot(spread, pairs, preferred_element_type=jnp.float32)
        return jnp.where(half, keys, 0.0).astype(jnp.bfloat16)

    meta_lane = lax.broadcasted_iota(jnp.int32, (4 * ROWS, 128), 1)
    meta = jnp.zeros((4 * ROWS, 128), jnp.float32)
    for request in range(2):
        start = count_ref[0] * request
        count = count_ref[request]
        blocks = (count + BLOCK - 1) // BLOCK
        doubles, single = blocks // 2, blocks % 2

        def slots(block, size):
            return [
                start + jnp.minimum(block * BLOCK + i, count - 1) for i in range(size * BLOCK)
            ]

        def latents(places):
            return jnp.concatenate([lat_ref[order_ref[p]] for p in places], axis=0)

        def score_blocks(size, block, maxima):
            places = slots(block, size)
            ropes = [rope_keys(places[i : i + SPREAD]) for i in range(0, len(places), SPREAD)]
            keys = jnp.concatenate([latents(places), jnp.concatenate(ropes, axis=0)], axis=1)
            lane = lax.broadcasted_iota(jnp.int32, (1, size * TOKENS), 1)
            limit = jnp.zeros((1, size * TOKENS), jnp.int32)
            for i, p in enumerate(places):
                valid = jnp.where(block * BLOCK + i < count, valid_ref[p], 0)
                limit = jnp.where(lane >= i * PAGE, i * PAGE + valid, limit)
            score = contract(query_ref[request], keys) * SCALE
            score = score + jnp.where(lane < limit, 0.0, NEG)
            for i in range(size):
                score_ref[block + i] = score[:, i * TOKENS : (i + 1) * TOKENS]
            for i in range(size * TOKENS // 128):
                maxima = jnp.maximum(maxima, score[:, i * 128 : (i + 1) * 128])
            return maxima

        def weigh_blocks(size, block, total):
            weight = [jnp.exp2(score_ref[block + i] - top) for i in range(size)]
            for part in weight:
                for i in range(TOKENS // 128):
                    total = total + part[:, i * 128 : (i + 1) * 128]
            weight = jnp.concatenate([w.astype(jnp.bfloat16) for w in weight], axis=1)
            acc_ref[...] += jnp.dot(
                weight, latents(slots(block, size)), preferred_element_type=jnp.float32
            )
            return total

        def over(step, carry):
            carry = lax.fori_loop(0, doubles, lambda i, c: step(2, 2 * i, c), carry)
            return lax.fori_loop(0, single, lambda i, c: step(1, 2 * doubles, c), carry)

        maxima = over(score_blocks, jnp.full((4 * ROWS, 128), NEG, jnp.float32))
        top = jnp.max(maxima, axis=1, keepdims=True)
        acc_ref[...] = jnp.zeros_like(acc_ref)
        total = over(weigh_blocks, jnp.zeros((4 * ROWS, 128), jnp.float32))
        total = jnp.sum(total, axis=1, keepdims=True)
        total = jnp.where(total > 0.0, total, 1.0)
        result = (acc_ref[...] / total).astype(jnp.bfloat16)
        for i, out in enumerate(outs):
            out[request * ROWS : (request + 1) * ROWS, :] = result[i * ROWS : (i + 1) * ROWS, :]
        rest = top + jnp.log2(total)
        for part in range(3):
            piece = rest.astype(jnp.bfloat16).astype(jnp.float32)
            meta = jnp.where(meta_lane == request * 3 + part, piece, meta)
            rest = rest - piece
    meta = meta.astype(jnp.bfloat16)
    for i, out in enumerate(outs):
        part = meta[i * ROWS : (i + 1) * ROWS, :]
        out[2 * ROWS :, :] = jnp.concatenate(
            [part[k * META : (k + 1) * META, :] for k in range(4)], axis=1
        )


def merge_kernel(p0, p1, p2, p3, fresh_ref, new_lat_ref, out_ref):
    parts = (p0, p1, p2, p3)
    meta = [
        jnp.concatenate(
            [p[2 * ROWS :, k * 128 : (k + 1) * 128] for k in range(4)], axis=0
        ).astype(jnp.float32)
        for p in parts
    ]
    for request in range(2):
        rows = slice(request * ROWS, (request + 1) * ROWS)
        sums = [
            m[:, 3 * request : 3 * request + 1]
            + m[:, 3 * request + 1 : 3 * request + 2]
            + m[:, 3 * request + 2 : 3 * request + 3]
            for m in meta
        ]
        fresh = [fresh_ref[request, :, step : step + 1] for step in range(2)]
        top = functools.reduce(jnp.maximum, sums + fresh)
        total = jnp.zeros((ROWS, 1), jnp.float32)
        acc = jnp.zeros((ROWS, 512), jnp.float32)
        for part, score in zip(parts, sums):
            weight = jnp.exp2(score - top)
            total = total + weight
            acc = acc + weight * part[rows, :].astype(jnp.float32)
        for step, score in enumerate(fresh):
            weight = jnp.exp2(score - top)
            total = total + weight
            key = new_lat_ref[request, step : step + 1, :].astype(jnp.float32)
            acc = acc + weight.astype(jnp.bfloat16).astype(jnp.float32) * key
        out_ref[request] = (acc / total).astype(jnp.bfloat16)


def fresh_scores(q_latent, q_rope, new_latent, new_rope):
    dims = (((3,), (2,)), ((0,), (0,)))
    score = lax.dot_general(q_latent, new_latent, dims, preferred_element_type=jnp.float32)
    score = score + lax.dot_general(q_rope, new_rope, dims, preferred_element_type=jnp.float32)
    step = jnp.arange(2, dtype=jnp.int32)
    seen = step[None, None, None, :] <= step[None, :, None, None]
    return jnp.where(seen, score * SCALE, NEG).reshape(2, ROWS, 2)


def page_table(row, pair):
    slot = jnp.arange(SLOTS, dtype=jnp.int32)
    owner_pair, a_from = slot // (2 * NX * NC), slot // (NX * NC) % 2
    x_from, c_from = slot // NC % NX, slot % NC
    y_from = serving_y(owner_pair, pair, c_from)
    holder = device_id(2 * pair + a_from, x_from, c_from, 0) // NY
    place = row[y_from * SLOTS + holder]
    request = place // 128
    length = jnp.where(
        request == 0, row[256] * 128 + row[258], row[257] * 128 + row[259]
    )
    valid = jnp.clip(length - (place % 128) * PAGE, 0, PAGE)
    key = jnp.where(valid > 0, request, 2)
    before = (key[None, :] < key[:, None]) | (
        (key[None, :] == key[:, None]) & (slot[None, :] < slot[:, None])
    )
    rank = jnp.sum(before.astype(jnp.int32), axis=1)
    hit = rank[:, None] == slot[None, :]
    order, valid = (jnp.sum(jnp.where(hit, v[:, None], 0), axis=0) for v in (slot, valid))
    count = jnp.stack([jnp.sum((key == r).astype(jnp.int32)) for r in range(2)])
    return order, valid, count


def on_device(
    latent_pages, rope_pages, page_place, lengths, q_latent, q_rope, new_latent, new_rope
):
    here = lax.axis_index("req")
    pair = here // (2 * NX * NC)
    place = page_place.astype(jnp.bfloat16)
    length = jnp.concatenate([lengths // 128, lengths % 128]).astype(jnp.bfloat16)
    row = jnp.pad(jnp.concatenate([place, length]), (0, 512 - 260))
    row = jnp.broadcast_to(row[None, :], (META, 512))
    rotary = q_rope.reshape(4, 2, META, ROPE).transpose(2, 0, 1, 3).reshape(META, 512)
    query = jnp.concatenate([q_latent.reshape(2 * ROWS, 512), rotary], axis=0)
    first = jnp.concatenate([query, row], axis=0)
    came = [
        lax.ppermute(query if d else first, AXES, [(t, s) for s, t in home_pairs(d)])
        for d in range(4)
    ]
    whole = pl.BlockSpec(memory_space=pltpu.VMEM)
    scalars = pl.BlockSpec(memory_space=pltpu.SMEM)
    exchange = functools.partial(
        lax.all_to_all,
        axis_name=AXES,
        split_axis=0,
        concat_axis=0,
        axis_index_groups=page_groups(),
        tiled=True,
    )
    lat = exchange(latent_pages)
    ropes = rope_pages.reshape(SLOTS, PAGE // 2, 2 * ROPE)
    lat, ropes = lax.optimization_barrier((lat, ropes))
    rope = exchange(ropes)
    queries = pl.pallas_call(
        query_kernel,
        out_shape=jax.ShapeDtypeStruct((2, 4 * ROWS, 512 + 2 * ROPE), jnp.bfloat16),
        in_specs=[whole] * 4,
        out_specs=whole,
        cost_estimate=pl.CostEstimate(flops=QCOST, bytes_accessed=2 << 20, transcendentals=0),
        compiler_params=pltpu.CompilerParams(vmem_limit_bytes=8 * 1024 * 1024),
        name="queries",
    )(*came)
    table = page_table(came[0][2 * ROWS + META].astype(jnp.int32), pair)
    partial = jax.ShapeDtypeStruct((2 * ROWS + META, 512), jnp.bfloat16)
    parts = pl.pallas_call(
        attend_kernel,
        out_shape=[partial] * 4,
        in_specs=[scalars] * 3 + [whole] * 3,
        out_specs=[whole] * 4,
        scratch_shapes=[
            pltpu.VMEM((SLOTS // BLOCK, 4 * ROWS, TOKENS), jnp.float32),
            pltpu.VMEM((4 * ROWS, 512), jnp.float32),
        ],
        compiler_params=pltpu.CompilerParams(vmem_limit_bytes=18 * 1024 * 1024),
        cost_estimate=pl.CostEstimate(
            flops=4 * ROWS * 6144 * 1152 * 2, bytes_accessed=8 << 20, transcendentals=1 << 20
        ),
        name="attend",
    )(*table, lat, rope, queries)
    home = [lax.ppermute(part, AXES, home_pairs(d)) for d, part in enumerate(parts)]
    out = pl.pallas_call(
        merge_kernel,
        out_shape=jax.ShapeDtypeStruct((2, ROWS, 512), jnp.bfloat16),
        in_specs=[whole] * 6,
        out_specs=whole,
        compiler_params=pltpu.CompilerParams(vmem_limit_bytes=4 * 1024 * 1024),
        name="merge",
    )(*home, fresh_scores(q_latent, q_rope, new_latent, new_rope), new_latent)
    return out.reshape(q_latent.shape)


def solution(mesh):
    return jax.shard_map(
        on_device,
        mesh=mesh,
        in_specs=(
            P(("req", "head"), None, None),
            P(("req", "head"), None),
            P("req"),
            P("req"),
            P("req", None, "head", None),
            P("req", None, "head", None),
            P("req", None, None),
            P("req", None, None),
        ),
        out_specs=P("req", None, "head", None),
        check_vma=False,
    )
```

```python
import functools
import math

import jax
import jax.numpy as jnp
from jax import lax
from jax.experimental import pallas as pl
from jax.experimental.pallas import tpu as pltpu
from jax.sharding import PartitionSpec as P

ROPE = 64
NOPE = 128
SCALE = float(NOPE + ROPE) ** -0.5 * math.log2(math.e)
NEG = -1e30

NZ, NX, NC, NY = 8, 4, 2, 4
AXES = ("req", "head")
PAIRS = NZ // 2
SLOTS = NZ * NX * NC
PAGE = 96
BLOCK = 8
SPREAD = 4
TOKENS = BLOCK * PAGE
ROWS = 64
META = 16
QCOST = 10**11


def device_id(z, x, core, y):
    return ((z * NX + x) * NC + core) * NY + y


def served_pair(pair, y, core):
    return (pair + (1 - 2 * core) * (y + 2 * (pair % 2))) % PAIRS


def serving_y(owner_pair, pair, core):
    return ((1 - 2 * core) * (owner_pair - pair) - 2 * (pair % 2)) % NY


def page_groups():
    return [
        [
            device_id(2 * j + zo % 2, x, c, serving_y(zo // 2, j, c))
            for zo in range(NZ)
            for x in range(NX)
            for c in range(NC)
        ]
        for j in range(PAIRS)
    ]


def home_pairs(d):
    return [
        (
            device_id(z, x, c, y),
            device_id(2 * served_pair(z // 2, y, c) + z % 2, x, c, (y + d) % NY),
        )
        for z in range(NZ)
        for x in range(NX)
        for c in range(NC)
        for y in range(NY)
    ]


def contract(left, right):
    return lax.dot_general(
        left, right, (((1,), (1,)), ((), ())), preferred_element_type=jnp.float32
    )


def query_kernel(q0, q1, q2, q3, out_ref):
    first = lax.broadcasted_iota(jnp.int32, (META, 2 * ROPE), 1) < ROPE
    for request in range(2):
        for i, query in enumerate((q0, q1, q2, q3)):
            rows = slice(i * ROWS, (i + 1) * ROWS)
            out_ref[request, rows, :512] = query[request * ROWS : (request + 1) * ROWS, :]
            for k in range(2):
                tile = slice((2 * request + k) * 128, (2 * request + k + 1) * 128)
                both = query[2 * ROWS : 2 * ROWS + META, tile].astype(jnp.float32)
                swapped = pltpu.roll(both, ROPE, 1)
                pair = (jnp.where(first, both, swapped), jnp.where(first, swapped, both))
                for h, part in enumerate(pair):
                    row = i * ROWS + k * 32 + h * META
                    out_ref[request, row : row + META, 512:] = part.astype(jnp.bfloat16)


def attend_kernel(
    order_ref, valid_ref, count_ref, lat_ref, rope_ref, query_ref,
    o0, o1, o2, o3, score_ref, acc_ref
):
    outs = (o0, o1, o2, o3)
    token = lax.broadcasted_iota(jnp.int32, (SPREAD * PAGE, SPREAD * PAGE // 2), 0)
    pair = lax.broadcasted_iota(jnp.int32, (SPREAD * PAGE, SPREAD * PAGE // 2), 1)
    spread = (token // 2 == pair).astype(jnp.bfloat16)
    half = (
        lax.broadcasted_iota(jnp.int32, (SPREAD * PAGE, 2 * ROPE), 0) % 2
        == lax.broadcasted_iota(jnp.int32, (SPREAD * PAGE, 2 * ROPE), 1) // ROPE
    )

    def rope_keys(places):
        pairs = jnp.concatenate([rope_ref[order_ref[p]] for p in places], axis=0)
        keys = jnp.dot(spread, pairs, preferred_element_type=jnp.float32)
        return jnp.where(half, keys, 0.0).astype(jnp.bfloat16)

    meta_lane = lax.broadcasted_iota(jnp.int32, (4 * ROWS, 128), 1)
    meta = jnp.zeros((4 * ROWS, 128), jnp.float32)
    for request in range(2):
        start = count_ref[0] * request
        count = count_ref[request]
        blocks = (count + BLOCK - 1) // BLOCK
        fours, double, single = blocks // 4, blocks // 2 % 2, blocks % 2

        def slots(block, size):
            return [
                start + jnp.minimum(block * BLOCK + i, count - 1) for i in range(size * BLOCK)
            ]

        def latents(places):
            return jnp.concatenate([lat_ref[order_ref[p]] for p in places], axis=0)

        def score_blocks(size, block, maxima):
            places = slots(block, size)
            ropes = [rope_keys(places[i : i + SPREAD]) for i in range(0, len(places), SPREAD)]
            keys = jnp.concatenate([latents(places), jnp.concatenate(ropes, axis=0)], axis=1)
            lane = lax.broadcasted_iota(jnp.int32, (1, size * TOKENS), 1)
            limit = jnp.zeros((1, size * TOKENS), jnp.int32)
            for i, p in enumerate(places):
                valid = jnp.where(block * BLOCK + i < count, valid_ref[p], 0)
                limit = jnp.where(lane >= i * PAGE, i * PAGE + valid, limit)
            score = contract(query_ref[request], keys) * SCALE
            score = score + jnp.where(lane < limit, 0.0, NEG)
            for i in range(size):
                score_ref[block + i] = score[:, i * TOKENS : (i + 1) * TOKENS]
            for i in range(size * TOKENS // 128):
                maxima = jnp.maximum(maxima, score[:, i * 128 : (i + 1) * 128])
            return maxima

        def weigh_blocks(size, block, total):
            weight = [jnp.exp2(score_ref[block + i] - top) for i in range(size)]
            for part in weight:
                for i in range(TOKENS // 128):
                    total = total + part[:, i * 128 : (i + 1) * 128]
            weight = jnp.concatenate([w.astype(jnp.bfloat16) for w in weight], axis=1)
            acc_ref[...] += jnp.dot(
                weight, latents(slots(block, size)), preferred_element_type=jnp.float32
            )
            return total

        def over(step, carry):
            carry = lax.fori_loop(0, fours, lambda i, c: step(4, 4 * i, c), carry)
            carry = lax.fori_loop(0, double, lambda i, c: step(2, 4 * fours, c), carry)
            return lax.fori_loop(0, single, lambda i, c: step(1, blocks - 1, c), carry)

        maxima = over(score_blocks, jnp.full((4 * ROWS, 128), NEG, jnp.float32))
        top = jnp.max(maxima, axis=1, keepdims=True)
        acc_ref[...] = jnp.zeros_like(acc_ref)
        total = over(weigh_blocks, jnp.zeros((4 * ROWS, 128), jnp.float32))
        total = jnp.sum(total, axis=1, keepdims=True)
        total = jnp.where(total > 0.0, total, 1.0)
        result = (acc_ref[...] / total).astype(jnp.bfloat16)
        for i, out in enumerate(outs):
            out[request * ROWS : (request + 1) * ROWS, :] = result[i * ROWS : (i + 1) * ROWS, :]
        rest = top + jnp.log2(total)
        for part in range(3):
            piece = rest.astype(jnp.bfloat16).astype(jnp.float32)
            meta = jnp.where(meta_lane == request * 3 + part, piece, meta)
            rest = rest - piece
    meta = meta.astype(jnp.bfloat16)
    for i, out in enumerate(outs):
        part = meta[i * ROWS : (i + 1) * ROWS, :]
        out[2 * ROWS :, :] = jnp.concatenate(
            [part[k * META : (k + 1) * META, :] for k in range(4)], axis=1
        )


def merge_kernel(p0, p1, p2, p3, fresh_ref, new_lat_ref, out_ref):
    parts = (p0, p1, p2, p3)
    meta = [
        jnp.concatenate(
            [p[2 * ROWS :, k * 128 : (k + 1) * 128] for k in range(4)], axis=0
        ).astype(jnp.float32)
        for p in parts
    ]
    for request in range(2):
        rows = slice(request * ROWS, (request + 1) * ROWS)
        sums = [
            m[:, 3 * request : 3 * request + 1]
            + m[:, 3 * request + 1 : 3 * request + 2]
            + m[:, 3 * request + 2 : 3 * request + 3]
            for m in meta
        ]
        fresh = [fresh_ref[request, :, step : step + 1] for step in range(2)]
        top = functools.reduce(jnp.maximum, sums + fresh)
        total = jnp.zeros((ROWS, 1), jnp.float32)
        acc = jnp.zeros((ROWS, 512), jnp.float32)
        for part, score in zip(parts, sums):
            weight = jnp.exp2(score - top)
            total = total + weight
            acc = acc + weight * part[rows, :].astype(jnp.float32)
        for step, score in enumerate(fresh):
            weight = jnp.exp2(score - top)
            total = total + weight
            key = new_lat_ref[request, step : step + 1, :].astype(jnp.float32)
            acc = acc + weight.astype(jnp.bfloat16).astype(jnp.float32) * key
        out_ref[request] = (acc / total).astype(jnp.bfloat16)


def fresh_scores(q_latent, q_rope, new_latent, new_rope):
    dims = (((3,), (2,)), ((0,), (0,)))
    score = lax.dot_general(q_latent, new_latent, dims, preferred_element_type=jnp.float32)
    score = score + lax.dot_general(q_rope, new_rope, dims, preferred_element_type=jnp.float32)
    step = jnp.arange(2, dtype=jnp.int32)
    seen = step[None, None, None, :] <= step[None, :, None, None]
    return jnp.where(seen, score * SCALE, NEG).reshape(2, ROWS, 2)


def page_table(row, pair):
    slot = jnp.arange(SLOTS, dtype=jnp.int32)
    owner_pair, a_from = slot // (2 * NX * NC), slot // (NX * NC) % 2
    x_from, c_from = slot // NC % NX, slot % NC
    y_from = serving_y(owner_pair, pair, c_from)
    holder = device_id(2 * pair + a_from, x_from, c_from, 0) // NY
    place = row[y_from * SLOTS + holder]
    request = place // 128
    length = jnp.where(
        request == 0, row[256] * 128 + row[258], row[257] * 128 + row[259]
    )
    valid = jnp.clip(length - (place % 128) * PAGE, 0, PAGE)
    key = jnp.where(valid > 0, request, 2)
    before = (key[None, :] < key[:, None]) | (
        (key[None, :] == key[:, None]) & (slot[None, :] < slot[:, None])
    )
    rank = jnp.sum(before.astype(jnp.int32), axis=1)
    hit = rank[:, None] == slot[None, :]
    order, valid = (jnp.sum(jnp.where(hit, v[:, None], 0), axis=0) for v in (slot, valid))
    count = jnp.stack([jnp.sum((key == r).astype(jnp.int32)) for r in range(2)])
    return order, valid, count


def on_device(
    latent_pages, rope_pages, page_place, lengths, q_latent, q_rope, new_latent, new_rope
):
    here = lax.axis_index("req")
    pair = here // (2 * NX * NC)
    place = page_place.astype(jnp.bfloat16)
    length = jnp.concatenate([lengths // 128, lengths % 128]).astype(jnp.bfloat16)
    row = jnp.pad(jnp.concatenate([place, length]), (0, 512 - 260))
    row = jnp.broadcast_to(row[None, :], (META, 512))
    rotary = q_rope.reshape(4, 2, META, ROPE).transpose(2, 0, 1, 3).reshape(META, 512)
    query = jnp.concatenate([q_latent.reshape(2 * ROWS, 512), rotary], axis=0)
    first = jnp.concatenate([query, row], axis=0)
    came = [
        lax.ppermute(query if d else first, AXES, [(t, s) for s, t in home_pairs(d)])
        for d in range(4)
    ]
    whole = pl.BlockSpec(memory_space=pltpu.VMEM)
    scalars = pl.BlockSpec(memory_space=pltpu.SMEM)
    exchange = functools.partial(
        lax.all_to_all,
        axis_name=AXES,
        split_axis=0,
        concat_axis=0,
        axis_index_groups=page_groups(),
        tiled=True,
    )
    lat = exchange(latent_pages)
    ropes = rope_pages.reshape(SLOTS, PAGE // 2, 2 * ROPE)
    lat, ropes = lax.optimization_barrier((lat, ropes))
    rope = exchange(ropes)
    queries = pl.pallas_call(
        query_kernel,
        out_shape=jax.ShapeDtypeStruct((2, 4 * ROWS, 512 + 2 * ROPE), jnp.bfloat16),
        in_specs=[whole] * 4,
        out_specs=whole,
        cost_estimate=pl.CostEstimate(flops=QCOST, bytes_accessed=2 << 20, transcendentals=0),
        compiler_params=pltpu.CompilerParams(vmem_limit_bytes=8 * 1024 * 1024),
        name="queries",
    )(*came)
    table = page_table(came[0][2 * ROWS + META].astype(jnp.int32), pair)
    partial = jax.ShapeDtypeStruct((2 * ROWS + META, 512), jnp.bfloat16)
    parts = pl.pallas_call(
        attend_kernel,
        out_shape=[partial] * 4,
        in_specs=[scalars] * 3 + [whole] * 3,
        out_specs=[whole] * 4,
        scratch_shapes=[
            pltpu.VMEM((SLOTS // BLOCK, 4 * ROWS, TOKENS), jnp.float32),
            pltpu.VMEM((4 * ROWS, 512), jnp.float32),
        ],
        compiler_params=pltpu.CompilerParams(vmem_limit_bytes=30 * 1024 * 1024),
        cost_estimate=pl.CostEstimate(
            flops=4 * ROWS * 6144 * 1152 * 2, bytes_accessed=8 << 20, transcendentals=1 << 20
        ),
        name="attend",
    )(*table, lat, rope, queries)
    home = [lax.ppermute(part, AXES, home_pairs(d)) for d, part in enumerate(parts)]
    out = pl.pallas_call(
        merge_kernel,
        out_shape=jax.ShapeDtypeStruct((2, ROWS, 512), jnp.bfloat16),
        in_specs=[whole] * 6,
        out_specs=whole,
        compiler_params=pltpu.CompilerParams(vmem_limit_bytes=4 * 1024 * 1024),
        name="merge",
    )(*home, fresh_scores(q_latent, q_rope, new_latent, new_rope), new_latent)
    return out.reshape(q_latent.shape)


def solution(mesh):
    return jax.shard_map(
        on_device,
        mesh=mesh,
        in_specs=(
            P(("req", "head"), None, None),
            P(("req", "head"), None),
            P("req"),
            P("req"),
            P("req", None, "head", None),
            P("req", None, "head", None),
            P("req", None, None),
            P("req", None, None),
        ),
        out_specs=P("req", None, "head", None),
        check_vma=False,
    )
```
